128 devices in a mesh: fsdp: 16 (over x, z_hi, core), seq: 8 (over z_lo, y).
Axes of the slice: x: 4, y: 4, z: 4 (z_hi: 2, z_lo: 2; z = z_hi * 2 + z_lo), core: 2. Of those that a mesh axis runs over, the one named last changes fastest.
Arguments:
- incoming_hidden_state: bfloat16 [16, 1024, 3072], P('fsdp', 'seq'), may hold values from -6 to 6
- projected_queries: bfloat16 [16, 1024, 3072], P('fsdp', 'seq'), may hold values from -120 to 120
- projected_keys: bfloat16 [16, 1024, 3072], P('fsdp', 'seq'), may hold values from -6.1 to 6.1
- projected_values: bfloat16 [16, 1024, 3072], P('fsdp', 'seq'), may hold values from -6 to 6
- training_noise: bfloat16 [16, 1024, 3072], P('fsdp', 'seq'), may hold values from -6 to 6
- group_trajectory_counts: int32 [4], replicated, may hold values from 1 to 8, 16 in all
- timestep: int32 [16], replicated, may hold values from 0 to 15
- block_shard_owner: int32 [16, 128, 1], P('fsdp', 'seq'), may hold values from 0 to 15; in each aligned block of 16 rows (0 to 15, 16 to 31, ..., all dimensions but the last counted through in order) at most 3 rows name the same one
- frozen_weight: bfloat16 [3072, 3072], P('fsdp'), may hold values from -0.109375 to 0.109375
- adapter_down_weight: bfloat16 [3072, 128], P('fsdp'), may hold values from -0.109375 to 0.109375
- adapter_up_weight: bfloat16 [3072, 128], P('fsdp'), may hold values from -0.5 to 0.5
- linear_reward_head: float32 [3072], replicated, may hold values from -0.109375 to 0.109375
Outputs:
- final: bfloat16 [16, 1024, 3072], P('fsdp', 'seq')
- grad_down: float32 [3072, 128], P(('fsdp', 'seq'))
- grad_up: float32 [3072, 128], P(('fsdp', 'seq'))
- device_token_loss: float32 [16, 8], P('fsdp', 'seq')
The draws below stay inside these ranges and needn't reach their ends.
Inputs may be any that keep to these rules, and one draw needn't show every extreme that they name: `block_shard_owner`: among the 16 blocks of one device at most 3 have the same owner, and exactly 3 in some device. `group_trajectory_counts`: they sum to 16; the largest is 8.
All inputs are finite; a program needn't handle non-finite values.
Results may differ from the reference program's by a relative error of at most 0.013.
Values may be sent and summed in bfloat16 or wider, within the bound.
A program may use at most 128 MiB of HBM per device.

```python
import math
import jax
import jax.numpy as jnp
import numpy as np
from jax import lax

HEADS = 24
HEAD_FEATURES = 128
ADAPTER_RANK = 128
TOKENS_DEV = 128
ROWS_PER_BLOCK = 8
SAMPLE_STEPS = 16
WINDOW_FEATURES = 3072
BLOCKS_DEV = 16
CAPACITY = 3
TRAJECTORIES = 16
LENGTH = 1024
TRAJECTORY_BLOCKS = 128
GROUPS = 4
GROUP_MOST = 8
N_FSDP = 16
N_SEQ = 8


def shared_keys(key):
    return jnp.clip(jax.random.normal(key, (TRAJECTORIES, LENGTH, WINDOW_FEATURES), jnp.float32), -6.0, 6.0)


def draw_projected_keys(key, part):
    shared = shared_keys(key)
    return shared.astype(jnp.bfloat16)


def draw_projected_queries(key, part):
    key = jax.random.fold_in(key, 32)
    fresh = jnp.clip(jax.random.normal(key, (TRAJECTORIES, LENGTH, WINDOW_FEATURES), jnp.float32), -6.0, 6.0)
    return fresh.astype(jnp.bfloat16)


def place_ends(array, rng, least, top_value):
    shape = array.shape
    place = [jax.random.randint(jax.random.fold_in(rng, axis), (), 0, shape[axis]) for axis in range(len(shape))]
    array = array.at[tuple(place)].set(least)
    longest = shape.index(max(shape))
    place[longest] = (place[longest] + 1) % shape[longest]
    return array.at[tuple(place)].set(top_value)


def shard_levels(rng, shape, pieces, least, top_value):
    def one(axis_at, blocks):
        steps = jax.random.uniform(jax.random.fold_in(jax.random.fold_in(rng, 6), axis_at), (blocks,), jnp.float32, least / len(pieces), top_value / len(pieces))
        return jnp.repeat(jnp.exp(steps), shape[axis_at] // blocks).reshape((-1,) + (1,) * (len(shape) - axis_at - 1))

    level = one(*pieces[0])
    for cut in pieces[1:]:
        level = level * one(*cut)
    return level


def split_up(amount, total, most, lean):
    portions = [(1 << 20) // math.isqrt(grade ** lean) + 1 for grade in range(2, amount + 1)]
    rest, given = total - most - (amount - 1), [1] * (amount - 1)
    while rest > 0:
        candidates = [i for i in range(amount - 1) if given[i] < most]
        whole, budget = sum([portions[i] for i in candidates]), rest
        for i in candidates:
            addition = min(most - given[i], max(1, budget * portions[i] // whole), rest)
            given[i] = given[i] + addition
            rest = rest - addition
    return np.array([most] + given)


def ragged_sizes(stream_key, count, total, most, lean):
    if count == 2:
        one = jax.random.randint(stream_key, (), max(1, total - most), min(most, total - 1) + 1)
        return jnp.stack([one, total - one])
    lengths = jnp.asarray(split_up(count, total, most, lean), jnp.int32)
    pairs = (count - 1) // 2
    giver, receiver = lengths[1:1 + 2 * pairs:2], lengths[2:2 + 2 * pairs:2]
    margin = jnp.minimum(giver - 1, most - receiver)
    shifted = jax.random.randint(jax.random.fold_in(stream_key, 1), (pairs,), 0, 1 << 20) % (margin + 1)
    lengths = lengths.at[1:1 + 2 * pairs:2].set(giver - shifted).at[2:2 + 2 * pairs:2].set(receiver + shifted)
    return lengths[jax.random.permutation(jax.random.fold_in(stream_key, 2), count)]


def shared_out(rng, own, number, rows, number_of, top, most, slope):
    order = jax.random.permutation(rng, number_of)
    heavy_load, common = load_shares(number_of, rows * top, most, slope, True), load_shares(number_of, rows * top, most, slope, False)
    places = jnp.arange(number_of)

    def named(lengths, rotation):
        used = int((lengths > 0).sum())
        fixed = max(1, used // 4)
        shifted = fixed + (places - fixed + rotation * (used - fixed)) % max(1, number_of - fixed)
        return jnp.zeros((number_of,), jnp.int32).at[order[jnp.where(places < fixed, places, shifted)]].set(jnp.asarray(lengths, jnp.int32))

    lengths = jnp.where(number % 4 == 0, named(heavy_load, number // 4), named(common, number - number // 4 - 1))
    mixed = jax.random.permutation(jax.random.fold_in(own, 3), number_of)
    donor, sink = mixed[0:number_of // 2 * 2:2], mixed[1:number_of // 2 * 2:2]
    room = jnp.minimum(lengths[donor] - 1, most - lengths[sink]) // 2
    room = jnp.where((donor == order[0]) | (sink == order[0]) | (lengths[sink] == 0), 0, jnp.maximum(room, 0))
    shifted = jax.random.randint(jax.random.fold_in(own, 4), (number_of // 2,), 0, 1 << 20) % (room + 1)
    lengths = lengths.at[donor].add(-shifted).at[sink].add(shifted)
    items = jnp.searchsorted(jnp.cumsum(lengths), jnp.arange(rows * top), side="right").astype(jnp.int32)
    listing = items.reshape(top, rows).T
    listing = listing[jax.random.permutation(jax.random.fold_in(own, 1), rows)]
    rotation = jax.random.randint(jax.random.fold_in(own, 2), (rows, 1), 0, top)
    return jnp.take_along_axis(listing, (jnp.arange(top)[None, :] + rotation) % top, axis=1)


def load_shares(count, total, most, skew, full):
    portions = [(1 << 20) // math.isqrt(rank ** skew) + 1 for rank in range(1, count + 1)]
    largest = most if full else min(most, max(-(-total // count), total * portions[0] // sum(portions)))
    least = 1 if total - largest >= count - 1 else 0
    given, rest = [largest] + [least] * (count - 1), total - largest - least * (count - 1)
    while rest > 0:
        candidates = [i for i in range(1, count) if given[i] < largest] or [i for i in range(1, count) if given[i] < most]
        mass, budget = sum([portions[i] for i in candidates]), rest
        for i in candidates:
            addition = min(most - given[i], max(1, budget * portions[i] // mass), rest)
            given[i] = given[i] + addition
            rest = rest - addition
    return np.array(given)


def noise(own_key, extent, scale, most, shards=(), dtype=jnp.bfloat16):
    level = shard_levels(own_key, extent, shards, -0.22, 0.18) if shards else 1.0
    array = jax.random.normal(own_key, extent, jnp.float32) * scale * level
    return jnp.minimum(jnp.maximum(array, -most), most).astype(dtype)


def setup_inputs(seed: int = 0) -> dict:
    streams_of = jax.random.split(jax.random.key(seed), 13)
    incoming_hidden_state = noise(streams_of[0], (TRAJECTORIES, LENGTH, WINDOW_FEATURES), 1.0, 6.0, ((0, 16), (1, 8)))
    projected_queries = draw_projected_queries(jax.random.fold_in(streams_of[12], 71), 0)
    projected_keys = draw_projected_keys(jax.random.fold_in(streams_of[12], 71), 0)
    projected_values = noise(streams_of[3], (TRAJECTORIES, LENGTH, WINDOW_FEATURES), 1.0, 6.0, ((0, 16), (1, 8)))
    training_noise = noise(streams_of[4], (TRAJECTORIES, LENGTH, WINDOW_FEATURES), 1.0, 6.0, ((0, 16), (1, 8)))
    group_trajectory_counts = ragged_sizes(streams_of[5], GROUPS, TRAJECTORIES, GROUP_MOST, 2).astype(jnp.int32)
    timestep = place_ends(jax.random.randint(streams_of[6], (TRAJECTORIES,), 0, SAMPLE_STEPS), jax.random.fold_in(streams_of[6], 1), 0, SAMPLE_STEPS - 1).astype(jnp.int32)
    block_shard_owner_keys = jax.random.split(jax.random.fold_in(streams_of[7], 1), TRAJECTORIES * TRAJECTORY_BLOCKS // BLOCKS_DEV)
    block_shard_owner_turns = jax.random.permutation(jax.random.fold_in(streams_of[7], 3), TRAJECTORIES * TRAJECTORY_BLOCKS // BLOCKS_DEV)
    block_shard_owner = jax.vmap(lambda own, number: shared_out(jax.random.fold_in(streams_of[7], 2), own, number, BLOCKS_DEV, N_FSDP, 1, CAPACITY, 2))(block_shard_owner_keys, block_shard_owner_turns).reshape((TRAJECTORIES, TRAJECTORY_BLOCKS, 1))
    frozen_weight = noise(streams_of[8], (WINDOW_FEATURES, WINDOW_FEATURES), WINDOW_FEATURES ** -0.5, 0.109375, ((0, 16),))
    adapter_down_weight = noise(streams_of[9], (WINDOW_FEATURES, ADAPTER_RANK), WINDOW_FEATURES ** -0.5, 0.109375, ((0, 16),))
    adapter_up_weight = noise(streams_of[10], (WINDOW_FEATURES, ADAPTER_RANK), ADAPTER_RANK ** -0.5, 0.5, ((0, 16),))
    linear_reward_head = noise(streams_of[11], (WINDOW_FEATURES,), WINDOW_FEATURES ** -0.5, 0.109375, (), jnp.float32)
    return dict(incoming_hidden_state=incoming_hidden_state, projected_queries=projected_queries, projected_keys=projected_keys, projected_values=projected_values, training_noise=training_noise, group_trajectory_counts=group_trajectory_counts, timestep=timestep, block_shard_owner=block_shard_owner, frozen_weight=frozen_weight, adapter_down_weight=adapter_down_weight, adapter_up_weight=adapter_up_weight, linear_reward_head=linear_reward_head)


adapter_scale = 2.0
adv_floor = 0.5
norm_eps = 1e-06

def noise_levels(timestep):
    level = 1.0 - timestep.astype(jnp.float32) / SAMPLE_STEPS
    return 5.0 * level / (1.0 + 4.0 * level)

def advantages(rewards, group_trajectory_counts):
    count_traj = rewards.shape[0]
    bounds = jnp.cumsum(group_trajectory_counts)
    members = lax.optimization_barrier(jnp.sum((bounds[None, :] <= jnp.arange(count_traj)[:, None]).astype(jnp.int32), axis=1))
    onehot = (members[:, None] == jnp.arange(group_trajectory_counts.shape[0])[None, :]).astype(jnp.float32)
    counts = lax.optimization_barrier(jnp.sum(onehot, axis=0))
    group_means = lax.optimization_barrier(jnp.sum(onehot * rewards[:, None], axis=0)) / counts
    spread = rewards - lax.optimization_barrier(jnp.sum(onehot * group_means[None, :], axis=1))
    variance = lax.optimization_barrier(jnp.sum(onehot * (spread * spread)[:, None], axis=0)) / counts
    deviation = lax.optimization_barrier(jnp.sum(onehot * jnp.sqrt(variance)[None, :], axis=1))
    return spread / jnp.maximum(deviation, adv_floor)

def attend(operands):
    queries, keys_in, values_in = operands
    seq_length = queries.shape[0]
    query_head_split = queries.reshape(seq_length, HEADS, HEAD_FEATURES).astype(jnp.float32)
    key_head_split = keys_in.reshape(seq_length, HEADS, HEAD_FEATURES).astype(jnp.float32)
    value_head_split = values_in.reshape(seq_length, HEADS, HEAD_FEATURES).astype(jnp.float32)
    attention_scores = jnp.einsum('buo,euo->ube', query_head_split, key_head_split) * (1.0 / math.sqrt(HEAD_FEATURES))
    row_max = lax.optimization_barrier(jnp.max(attention_scores, axis=2, keepdims=True))
    expo = jnp.exp(attention_scores - row_max)
    total = lax.optimization_barrier(jnp.sum(expo, axis=2))
    rounded_value = lax.optimization_barrier(expo.astype(jnp.bfloat16))
    blended_latent = jnp.einsum('xfc,cxq->fxq', rounded_value.astype(jnp.float32), value_head_split)
    blended_latent = blended_latent / jnp.transpose(total)[:, :, None]
    return blended_latent.reshape(seq_length, WINDOW_FEATURES)

def reference(incoming_hidden_state, projected_queries, projected_keys, projected_values, training_noise, group_trajectory_counts, timestep, block_shard_owner, frozen_weight, adapter_down_weight, adapter_up_weight, linear_reward_head):
    attention = lax.map(attend, (projected_queries, projected_keys, projected_values))
    final = (incoming_hidden_state.astype(jnp.float32) + attention).astype(jnp.bfloat16)
    rewards = lax.optimization_barrier(jnp.sum(final.astype(jnp.float32) * linear_reward_head[None, None, :], axis=(1, 2))) / math.sqrt(LENGTH)
    advantage = advantages(rewards, group_trajectory_counts)
    sigma = noise_levels(timestep)
    device_total = N_FSDP * N_SEQ
    seq_of_block = (jnp.arange(TRAJECTORY_BLOCKS) // BLOCKS_DEV).astype(jnp.int32)

    def train_one(totals, operands):
        latent, fresh, level, weight, owner = operands
        latent_f = latent.astype(jnp.float32)
        fresh_f = fresh.astype(jnp.float32)
        noised_latent = ((1.0 - level) * latent_f + level * fresh_f).astype(jnp.bfloat16)
        target = fresh_f - latent_f
        frozen_output = jnp.dot(noised_latent, frozen_weight, preferred_element_type=jnp.float32)
        rank_projection = jnp.dot(noised_latent, adapter_down_weight, preferred_element_type=jnp.float32).astype(jnp.bfloat16)
        predicted_velocity = frozen_output + adapter_scale * jnp.dot(rank_projection, jnp.transpose(adapter_up_weight), preferred_element_type=jnp.float32)
        error = predicted_velocity - target
        token_loss = weight * lax.optimization_barrier(jnp.mean(error * error, axis=1))
        velocity_target = (weight * error / LENGTH).astype(jnp.bfloat16)
        backward_pass = (adapter_scale * jnp.dot(velocity_target, adapter_up_weight, preferred_element_type=jnp.float32)).astype(jnp.bfloat16)
        noisy_blocks = noised_latent.reshape(TRAJECTORY_BLOCKS, ROWS_PER_BLOCK, WINDOW_FEATURES).astype(jnp.float32)
        backward_block_list = backward_pass.reshape(TRAJECTORY_BLOCKS, ROWS_PER_BLOCK, ADAPTER_RANK).astype(jnp.float32)
        velocity_block_list = velocity_target.reshape(TRAJECTORY_BLOCKS, ROWS_PER_BLOCK, WINDOW_FEATURES).astype(jnp.float32)
        rank_block_list = rank_projection.reshape(TRAJECTORY_BLOCKS, ROWS_PER_BLOCK, ADAPTER_RANK).astype(jnp.float32)
        block_down = jnp.einsum('gyw,gyh->gwh', noisy_blocks, backward_block_list)
        block_up_weight = adapter_scale * jnp.einsum('gyw,gyh->gwh', velocity_block_list, rank_block_list)
        per_block = jnp.concatenate([block_down, block_up_weight], axis=2)
        device_of = (owner[:, 0] * N_SEQ + seq_of_block).astype(jnp.int32)
        totals = totals + jax.ops.segment_sum(per_block, device_of, num_segments=device_total)
        block_loss = lax.optimization_barrier(jnp.sum(token_loss.reshape(TRAJECTORY_BLOCKS, ROWS_PER_BLOCK), axis=1))
        return (totals, block_loss)
    zero_filled = jnp.zeros((device_total, WINDOW_FEATURES, 2 * ADAPTER_RANK), jnp.float32)
    shard_grads, block_loss = lax.scan(train_one, zero_filled, (final, training_noise, sigma, advantage, block_shard_owner))
    norm_sq = lax.optimization_barrier(jnp.sum(shard_grads * shard_grads, axis=(1, 2)))
    norms = jnp.sqrt(norm_sq)
    limit = jnp.sqrt(jnp.mean(norm_sq) + norm_eps)
    clip_gradient = limit / jnp.maximum(norms, limit)
    gradient_list = lax.optimization_barrier(jnp.sum(clip_gradient[:, None, None] * shard_grads, axis=0))
    owners = block_shard_owner.reshape(TRAJECTORIES, N_SEQ, BLOCKS_DEV)
    owner_hot = (owners[..., None] == jnp.arange(N_FSDP)[None, None, None, :]).astype(jnp.float32)
    device_token_loss = jnp.einsum('bsk,bskt->ts', block_loss.reshape(TRAJECTORIES, N_SEQ, BLOCKS_DEV), owner_hot) / TOKENS_DEV
    return (final, gradient_list[:, :ADAPTER_RANK], gradient_list[:, ADAPTER_RANK:], device_token_loss)
```

```python
import functools
import math

import jax
import jax.numpy as jnp
from jax import lax
from jax.experimental import pallas as pl
from jax.experimental.pallas import tpu as pltpu
from jax.sharding import PartitionSpec as P

MESH = pl.DeviceIdType.MESH
BF16 = jnp.bfloat16
F32 = jnp.float32

HEAD = 128
ROWS_PER_BLOCK = 8
SAMPLE_STEPS = 16
RANK = 128

adapter_scale = 2.0
adv_floor = 0.5
norm_eps = 1e-06


def noise_levels(timestep):
    level = 1.0 - timestep.astype(jnp.float32) / SAMPLE_STEPS
    return 5.0 * level / (1.0 + 4.0 * level)


def advantages(rewards, group_trajectory_counts):
    count_traj = rewards.shape[0]
    bounds = jnp.cumsum(group_trajectory_counts)
    members = jnp.sum(
        (bounds[None, :] <= jnp.arange(count_traj)[:, None]).astype(jnp.int32), axis=1
    )
    onehot = (members[:, None] == jnp.arange(group_trajectory_counts.shape[0])[None, :]).astype(
        jnp.float32
    )
    counts = jnp.sum(onehot, axis=0)
    group_means = jnp.sum(onehot * rewards[:, None], axis=0) / counts
    spread = rewards - jnp.sum(onehot * group_means[None, :], axis=1)
    variance = jnp.sum(onehot * (spread * spread)[:, None], axis=0) / counts
    deviation = jnp.sum(onehot * jnp.sqrt(variance)[None, :], axis=1)
    return spread / jnp.maximum(deviation, adv_floor)


def enter(groups):
    barrier = pltpu.get_barrier_semaphore()
    total = 0
    for axis, count in groups:
        me = lax.axis_index(axis)
        for offset in range(1, count):
            peer = lax.rem(me + offset, count)
            pl.semaphore_signal(barrier, inc=1, device_id={axis: peer}, device_id_type=MESH)
            total += 1
    pl.semaphore_wait(barrier, total)


def remote(src, dst, send, recv, axis, peer):
    return pltpu.make_async_remote_copy(
        src_ref=src, dst_ref=dst, send_sem=send, recv_sem=recv,
        device_id={axis: peer}, device_id_type=MESH,
    )


def share(axis, count, src, slots, send, recv):
    me = lax.axis_index(axis)
    copies = []
    for offset in range(1, count):
        peer = lax.rem(me + offset, count)
        copy = remote(src, slots.at[me], send.at[offset], recv.at[offset], axis, peer)
        copy.start()
        copies.append(copy)
    slots[me] = src[...]
    return copies


def finish(copies):
    for copy in copies:
        copy.wait()


def attend_kernel(
    n_seq, n_fsdp, q, k, v, hidden, head, final, rewards,
    qa, ka, va, oa, ar, mine, slots, send, recv, local, bsend, brecv,
    s1, r1, s2, r2,
):
    s = lax.axis_index("seq")
    rows = q.shape[0]
    width = q.shape[1] // n_seq
    length = rows * n_seq
    heads = width // HEAD
    enter((("seq", n_seq), ("fsdp", n_fsdp)))

    def cols(i):
        return pl.ds(pl.multiple_of(i * width, 128), width)

    def rws(i):
        return pl.ds(pl.multiple_of(i * rows, 128), rows)

    copies = []
    for j, (src, dst) in enumerate(((k, ka), (q, qa), (v, va))):
        for offset in range(1, n_seq):
            peer = lax.rem(s + offset, n_seq)
            copy = remote(src.at[:, cols(peer)], dst.at[rws(s), :], send.at[j, offset],
                          recv.at[j, offset], "seq", peer)
            copy.start()
            copies.append(copy)
        own = pltpu.make_async_copy(src.at[:, cols(s)], dst.at[rws(s), :], local.at[j])
        own.start()
        copies.append(own)
    finish(copies)

    factor = math.log2(math.e) / math.sqrt(HEAD)
    pairs = n_seq // 2

    def block(j):
        at = pl.ds(pl.multiple_of(j * 2 * rows, 128), 2 * rows)
        for h in range(heads):
            here = slice(h * HEAD, (h + 1) * HEAD)
            scores = lax.dot_general(qa[at, here], ka[:, here], (((1,), (1,)), ((), ())),
                                     preferred_element_type=F32)
            top = jnp.max(scores, axis=1, keepdims=True)
            expo = jnp.exp2((scores - top) * factor)
            total = jnp.sum(expo, axis=1, keepdims=True)
            out = jnp.dot(expo.astype(BF16), va[:, here], preferred_element_type=F32) / total
            oa[at, here] = out.astype(BF16)

    def back(peer):
        offset = lax.rem(peer - s + n_seq, n_seq)
        return remote(oa.at[rws(peer), :], ar.at[:, cols(s)], bsend.at[offset], brecv.at[offset],
                      "seq", peer)

    for i in range(pairs):
        j = lax.rem(s // 2 + 1 + i, pairs)
        block(j)
        if i < pairs - 1:
            for half in range(2):
                back(2 * j + half).start()
        else:
            back(s + 1 - 2 * lax.rem(s, 2)).start()
    ar[:, cols(s)] = oa[rws(s), :]
    for offset in range(1, n_seq):
        back(lax.rem(s + offset, n_seq)).wait()

    reward = jnp.zeros((1, 1), F32)
    for c in range(n_seq):
        here = slice(c * width, (c + 1) * width)
        value = (hidden[:, here].astype(F32) + ar[:, here].astype(F32)).astype(BF16)
        final[:, here] = value
        part = jnp.sum(value.astype(F32) * head[:, here], axis=0, keepdims=True)
        reward = reward + jnp.sum(part, axis=1, keepdims=True)
    mine[...] = jnp.broadcast_to(reward / math.sqrt(length), mine.shape)
    finish(share("seq", n_seq, mine, slots, s1, r1))
    total = slots[0]
    for c in range(1, n_seq):
        total = total + slots[c]
    mine[...] = total
    finish(share("fsdp", n_fsdp, mine, rewards, s2, r2))


def attend(q, k, v, hidden, head, n_seq, n_fsdp):
    rows, features = q.shape
    width = features // n_seq
    vmem = pl.BlockSpec(memory_space=pltpu.VMEM)
    hbm = pl.BlockSpec(memory_space=pl.ANY)
    dma = pltpu.SemaphoreType.DMA
    return pl.pallas_call(
        functools.partial(attend_kernel, n_seq, n_fsdp),
        out_shape=(
            jax.ShapeDtypeStruct((rows, features), BF16),
            jax.ShapeDtypeStruct((n_fsdp, 8, 128), F32),
        ),
        in_specs=[hbm, hbm, hbm, vmem, vmem],
        out_specs=(vmem, vmem),
        scratch_shapes=[
            pltpu.VMEM((rows * n_seq, width), BF16),
            pltpu.VMEM((rows * n_seq, width), BF16),
            pltpu.VMEM((rows * n_seq, width), BF16),
            pltpu.VMEM((rows * n_seq, width), BF16),
            pltpu.VMEM((rows, features), BF16),
            pltpu.VMEM((8, 128), F32),
            pltpu.VMEM((n_seq, 8, 128), F32),
            dma((3, n_seq)), dma((3, n_seq)), dma((3,)),
            dma((n_seq,)), dma((n_seq,)),
            dma((n_seq,)), dma((n_seq,)),
            dma((n_fsdp,)), dma((n_fsdp,)),
        ],
        compiler_params=pltpu.CompilerParams(
            collective_id=0, has_side_effects=True, vmem_limit_bytes=40 * 2**20
        ),
        cost_estimate=pl.CostEstimate(flops=2 * 10**9, bytes_accessed=5 * 2**20, transcendentals=3 * 2**20),
    )(q, k, v, hidden, head)


def grads_kernel(
    n_seq, n_fsdp, noisy, slope, lows, meta, down_out, up_out, loss_out,
    nt, st, na, sa, la, ma, left, sh, mine, slots1, slots2, gt, gslots,
    send, recv, s1, r1, s2, r2, s3, r3,
):
    t = lax.axis_index("fsdp")
    s = lax.axis_index("seq")
    rows, features = noisy.shape
    width = features // n_fsdp
    own = width // n_seq
    enter((("fsdp", n_fsdp), ("seq", n_seq)))

    for c in range(features // 128):
        here = slice(c * 128, (c + 1) * 128)
        nt[here, :] = noisy[:, here].T
        st[here, :] = slope[:, here].T

    def feat(i):
        return pl.ds(pl.multiple_of(i * width, 16), width)

    def toks(i):
        return pl.ds(pl.multiple_of(i * rows, 128), rows)

    copies = []
    for offset in range(1, n_fsdp):
        peer = lax.rem(t + offset, n_fsdp)
        for j, (src, dst) in enumerate((
            (nt.at[feat(peer), :], na.at[:, toks(t)]),
            (st.at[feat(peer), :], sa.at[:, toks(t)]),
            (lows, la.at[:, toks(t)]),
            (meta, ma.at[:, toks(t)]),
        )):
            copy = remote(src, dst, send.at[j, offset], recv.at[j, offset], "fsdp", peer)
            copy.start()
            copies.append(copy)
    na[:, toks(t)] = nt[feat(t), :]
    sa[:, toks(t)] = st[feat(t), :]
    la[:, toks(t)] = lows[...]
    ma[:, toks(t)] = meta[...]
    finish(copies)

    owner = ma[0:1, :]
    loss = ma[1:2, :]
    loss_out[...] = jnp.broadcast_to(
        jnp.sum(jnp.where(owner == t.astype(F32), loss, 0.0), axis=1, keepdims=True), loss_out.shape
    )
    lane = lax.broadcasted_iota(jnp.int32, (8, 128), 1)
    norms = jnp.zeros((8, 128), F32)
    batch = 4
    for g in range(n_fsdp // batch):
        for e in range(batch):
            hot = jnp.where(owner == float(g * batch + e), 1.0, 0.0)
            hot = jnp.broadcast_to(hot, (16, owner.shape[1])).astype(BF16)
            for j in range(2):
                for r in range(RANK // 16):
                    left[j, e * RANK + r * 16:e * RANK + r * 16 + 16, :] = (
                        la[j * RANK + r * 16:j * RANK + r * 16 + 16, :] * hot
                    )
        for j, other in enumerate((na, sa)):
            prod = lax.dot_general(left[j], other[...], (((1,), (1,)), ((), ())),
                                   preferred_element_type=F32)
            if j == 1:
                prod = adapter_scale * prod
            for e in range(batch):
                piece = prod[e * RANK:(e + 1) * RANK]
                d = g * batch + e
                sh[d, j * RANK:(j + 1) * RANK, :] = piece
                square = jnp.sum(jnp.sum(piece * piece, axis=0, keepdims=True), axis=1, keepdims=True)
                norms = jnp.where(lane == d, norms + square, norms)
    mine[...] = norms
    finish(share("fsdp", n_fsdp, mine, slots1, s1, r1))
    norms = slots1[0]
    for c in range(1, n_fsdp):
        norms = norms + slots1[c]
    mine[...] = norms
    finish(share("seq", n_seq, mine, slots2, s2, r2))
    every = slots2[0]
    for c in range(1, n_seq):
        every = every + slots2[c]
    square_total = jnp.sum(every[0:1, :], axis=1, keepdims=True)
    limit = jnp.sqrt(square_total / (n_fsdp * n_seq) + norm_eps)
    clip = limit / jnp.maximum(jnp.sqrt(norms[0:1, :]), limit)
    lane1 = lax.broadcasted_iota(jnp.int32, (1, 128), 1)
    factors = [jnp.sum(jnp.where(lane1 == d, clip, 0.0), axis=1, keepdims=True) for d in range(n_fsdp)]
    for j in range(2):
        here = slice(j * RANK, (j + 1) * RANK)
        total = factors[0] * sh[0, here, :]
        for d in range(1, n_fsdp):
            total = total + factors[d] * sh[d, here, :]
        gt[:, here] = total.T

    copies = []
    for offset in range(1, n_seq):
        peer = lax.rem(s + offset, n_seq)
        copy = remote(gt.at[pl.ds(pl.multiple_of(peer * own, 8), own), :], gslots.at[s],
                      s3.at[offset], r3.at[offset], "seq", peer)
        copy.start()
        copies.append(copy)
    gslots[s] = gt[pl.ds(pl.multiple_of(s * own, 8), own), :]
    finish(copies)
    total = gslots[0]
    for c in range(1, n_seq):
        total = total + gslots[c]
    down_out[...] = total[:, :RANK]
    up_out[...] = total[:, RANK:]


def grads(noisy, slope, lows, meta, n_seq, n_fsdp):
    rows, features = noisy.shape
    width = features // n_fsdp
    own = width // n_seq
    every = rows * n_fsdp
    vmem = pl.BlockSpec(memory_space=pltpu.VMEM)
    dma = pltpu.SemaphoreType.DMA
    return pl.pallas_call(
        functools.partial(grads_kernel, n_seq, n_fsdp),
        out_shape=(
            jax.ShapeDtypeStruct((own, RANK), F32),
            jax.ShapeDtypeStruct((own, RANK), F32),
            jax.ShapeDtypeStruct((8, 128), F32),
        ),
        in_specs=[vmem] * 4,
        out_specs=(vmem,) * 3,
        scratch_shapes=[
            pltpu.VMEM((features, rows), BF16),
            pltpu.VMEM((features, rows), BF16),
            pltpu.VMEM((width, every), BF16),
            pltpu.VMEM((width, every), BF16),
            pltpu.VMEM((2 * RANK, every), BF16),
            pltpu.VMEM((8, every), F32),
            pltpu.VMEM((2, 4 * RANK, every), BF16),
            pltpu.VMEM((n_fsdp, 2 * RANK, width), F32),
            pltpu.VMEM((8, 128), F32),
            pltpu.VMEM((n_fsdp, 8, 128), F32),
            pltpu.VMEM((n_seq, 8, 128), F32),
            pltpu.VMEM((width, 2 * RANK), F32),
            pltpu.VMEM((n_seq, own, 2 * RANK), F32),
            dma((4, n_fsdp)), dma((4, n_fsdp)),
            dma((n_fsdp,)), dma((n_fsdp,)),
            dma((n_seq,)), dma((n_seq,)),
            dma((n_seq,)), dma((n_seq,)),
        ],
        compiler_params=pltpu.CompilerParams(
            collective_id=1, has_side_effects=True, vmem_limit_bytes=40 * 2**20
        ),
        cost_estimate=pl.CostEstimate(flops=4 * 10**9, bytes_accessed=2 * 2**20, transcendentals=0),
    )(noisy, slope, lows, meta)


def per_device(
    incoming_hidden_state, projected_queries, projected_keys, projected_values, training_noise,
    group_trajectory_counts, timestep, block_shard_owner, frozen_weight, adapter_down_weight,
    adapter_up_weight, linear_reward_head,
):
    rows, features = incoming_hidden_state.shape[1:]
    n_seq = lax.axis_size("seq")
    n_fsdp = lax.axis_size("fsdp")
    length = rows * n_seq
    t = lax.axis_index("fsdp")
    frozen = lax.all_gather(frozen_weight, "fsdp", axis=0, tiled=True)
    adapters = lax.all_gather(
        jnp.concatenate([adapter_down_weight, adapter_up_weight], axis=1), "fsdp", axis=0, tiled=True
    )
    down_weight, up_weight = adapters[:, :RANK], adapters[:, RANK:]
    final, slots = attend(
        projected_queries[0], projected_keys[0], projected_values[0], incoming_hidden_state[0],
        linear_reward_head[None, :], n_seq, n_fsdp,
    )
    advantage = advantages(slots[:, 0, 0], group_trajectory_counts)[t]
    level = noise_levels(timestep)[t]
    latent = final.astype(F32)
    fresh = training_noise[0].astype(F32)
    noisy = ((1.0 - level) * latent + level * fresh).astype(BF16)
    target = fresh - latent
    lowrank = jnp.dot(noisy, down_weight, preferred_element_type=F32).astype(BF16)
    error = (
        jnp.dot(noisy, frozen, preferred_element_type=F32)
        + adapter_scale * lax.dot_general(lowrank, up_weight, (((1,), (1,)), ((), ())),
                                          preferred_element_type=F32)
        - target
    )
    token_loss = advantage * jnp.mean(error * error, axis=1) / rows
    slope = (advantage * error / length).astype(BF16)
    back = (adapter_scale * jnp.dot(slope, up_weight, preferred_element_type=F32)).astype(BF16)
    lows = jnp.concatenate([back.T, lowrank.T], axis=0)
    owners = jnp.repeat(block_shard_owner[0, :, 0], ROWS_PER_BLOCK).astype(F32)
    meta = jnp.concatenate([owners[None], token_loss[None], jnp.zeros((6, rows), F32)], axis=0)
    grad_down, grad_up, loss = grads(noisy, slope, lows, meta, n_seq, n_fsdp)
    return final[None], grad_down, grad_up, loss[:1, :1]


def solution(mesh):
    return jax.shard_map(
        per_device,
        mesh=mesh,
        in_specs=(
            P("fsdp", "seq", None),
            P("fsdp", "seq", None),
            P("fsdp", "seq", None),
            P("fsdp", "seq", None),
            P("fsdp", "seq", None),
            P(),
            P(),
            P("fsdp", "seq", None),
            P("fsdp", None),
            P("fsdp", None),
            P("fsdp", None),
            P(),
        ),
        out_specs=(
            P("fsdp", "seq", None),
            P(("fsdp", "seq"), None),
            P(("fsdp", "seq"), None),
            P("fsdp", "seq"),
        ),
        check_vma=False,
    )
```

```python
import functools
import math

import jax
import jax.numpy as jnp
from jax import lax
from jax.experimental import pallas as pl
from jax.experimental.pallas import tpu as pltpu
from jax.sharding import PartitionSpec as P

MESH = pl.DeviceIdType.MESH
BF16 = jnp.bfloat16
F32 = jnp.float32

HEAD = 128
ROWS_PER_BLOCK = 8
SAMPLE_STEPS = 16
RANK = 128
SPLIT = 1792

adapter_scale = 2.0
adv_floor = 0.5
norm_eps = 1e-06


def remote(src, dst, send, recv, axis, peer):
    return pltpu.make_async_remote_copy(
        src_ref=src, dst_ref=dst, send_sem=send, recv_sem=recv,
        device_id={axis: peer}, device_id_type=MESH,
    )


def share(axis, count, src, slots, send, recv):
    me = lax.axis_index(axis)
    copies = []
    for offset in range(1, count):
        peer = lax.rem(me + offset, count)
        copy = remote(src, slots.at[me], send.at[offset], recv.at[offset], axis, peer)
        copy.start()
        copies.append(copy)
    slots[me] = src[...]
    return copies


def finish(copies):
    for copy in copies:
        copy.wait()


def advantage_row(counts, rewards, lane):
    result = jnp.zeros_like(rewards)
    low = jnp.int32(0)
    for g in range(counts.shape[0]):
        high = low + counts[g]
        inside = jnp.where((lane >= low) & (lane < high), 1.0, 0.0)
        number = jnp.sum(inside, axis=1, keepdims=True)
        mean = jnp.sum(inside * rewards, axis=1, keepdims=True) / number
        dev = inside * (rewards - mean)
        spread = jnp.sqrt(jnp.sum(dev * dev, axis=1, keepdims=True) / number)
        result = result + dev / jnp.maximum(spread, adv_floor)
        low = high
    return result


def step_kernel(
    n_seq, n_fsdp,
    hidden_in, q, k, v, noise_in, counts, steps, owners, frozen, down, up, head,
    final, down_out, up_out, loss_out,
    hidden, noise, wb, qa, ka, va, oa, ar, noisy, acc, nt, st, na, sa, la, ma, left, sh,
    mine, meta, lows, rslots, rewards, slots1, slots2, gt, gslots,
    ksend, krecv, klocal, wsend, wrecv, bsend, brecv, r1s, r1r, r2s, r2r,
    send, recv, s1, r1, s2, r2, s3, r3,
):
    t = lax.axis_index("fsdp")
    s = lax.axis_index("seq")
    rows, features = q.shape
    width = features // n_seq
    length = rows * n_seq
    heads = width // HEAD
    nr = frozen.shape[0]
    nc = wb.shape[1]
    own = nr // n_seq
    x, zh, core = t // 4, lax.rem(t // 2, 2), lax.rem(t, 2)
    xp, xm, xo, zz = lax.rem(x + 1, 4), lax.rem(x + 3, 4), lax.rem(x + 2, 4), 1 - zh

    def place(a, b):
        return a * 4 + b * 2 + core

    dev_xp, dev_xm = (place(xp, zh), s), (place(xm, zh), s)
    dev_z = (place(x, zz), lax.rem(s + n_seq // 2, n_seq))
    dev_core = (x * 4 + zh * 2 + 1 - core, s)

    barrier = pltpu.get_barrier_semaphore()
    for axis, count, me in (("seq", n_seq, s), ("fsdp", n_fsdp, t)):
        for offset in range(1, count):
            pl.semaphore_signal(barrier, inc=1, device_id={axis: lax.rem(me + offset, count)},
                                device_id_type=MESH)
    pl.semaphore_signal(barrier, inc=1, device_id=dev_z, device_id_type=MESH)

    def span(i, size):
        return pl.ds(pl.multiple_of(i * size, 128), size)

    def feat(i):
        return pl.ds(pl.multiple_of(i * nr, 16), nr)

    wlocal = []
    for j, (part, at, size) in enumerate(((frozen, 0, features), (down, features, RANK),
                                          (up, features + RANK, RANK))):
        wlocal.append(pltpu.make_async_copy(part, wb.at[feat(t), pl.ds(at, size)], klocal.at[j]))
    klocals = []
    for j, (part, dst) in enumerate(((k, ka), (q, qa), (v, va))):
        klocals.append(pltpu.make_async_copy(part.at[:, span(s, width)], dst.at[span(s, rows), :],
                                             klocal.at[3 + j]))
    hlocal = [pltpu.make_async_copy(hidden_in, hidden, klocal.at[6]),
              pltpu.make_async_copy(noise_in, noise, klocal.at[7])]
    for copy in wlocal + klocals + hlocal:
        copy.start()
    pl.semaphore_wait(barrier, n_seq + n_fsdp - 1)

    kcopies = []

    def scatter(j, part, dst):
        for offset in range(1, n_seq):
            peer = lax.rem(s + offset, n_seq)
            copy = remote(part.at[:, span(peer, width)], dst.at[span(s, rows), :],
                          ksend.at[j, offset], krecv.at[j, offset], "seq", peer)
            copy.start()
            kcopies.append(copy)

    half = nr // 2
    whole, first, second = (0, nr), (0, half), (half, half)
    every, near, far = (0, nc), (0, SPLIT), (SPLIT, nc - SPLIT)
    wcopies = {}

    def pass_on(i, block, part, columns, device):
        ref = wb.at[pl.ds(pl.multiple_of(block * nr + part[0], 16), part[1]),
                    pl.ds(columns[0], columns[1])]
        wcopies[i] = pltpu.make_async_remote_copy(
            src_ref=ref, dst_ref=ref, send_sem=wsend.at[i], recv_sem=wrecv.at[i],
            device_id=device, device_id_type=MESH)
        wcopies[i].start()

    def arrived(*which):
        for i in which:
            wcopies[i].wait_recv()

    scatter(0, k, ka)
    finish(wlocal)
    pass_on(0, t, whole, every, dev_xp)
    pass_on(1, t, whole, every, dev_xm)
    pass_on(2, t, whole, every, dev_z)
    pass_on(3, t, whole, every, dev_core)
    scatter(1, q, qa)
    scatter(2, v, va)

    arrived(0, 1, 2)
    pass_on(4, place(xm, zh), first, every, dev_xp)
    pass_on(5, place(xp, zh), second, every, dev_xm)
    pass_on(8, place(xm, zh), whole, far, dev_z)
    pass_on(9, place(xp, zh), whole, far, dev_z)
    pass_on(6, place(x, zz), whole, near, dev_xp)
    pass_on(7, place(x, zz), whole, near, dev_xm)
    pass_on(10, place(xm, zh), whole, every, dev_core)
    pass_on(11, place(xp, zh), whole, every, dev_core)
    pass_on(12, place(x, zz), whole, every, dev_core)

    finish(klocals + kcopies)
    factor = math.log2(math.e) / math.sqrt(HEAD)
    pairs = n_seq // 2

    def back_copy(peer):
        offset = lax.rem(peer - s + n_seq, n_seq)
        return remote(oa.at[span(peer, rows), :], ar.at[:, span(s, width)], bsend.at[offset],
                      brecv.at[offset], "seq", peer)

    for i in range(pairs):
        j = lax.rem(s // 2 + 1 + i, pairs)
        at = span(j, 2 * rows)
        for h in range(heads):
            here = slice(h * HEAD, (h + 1) * HEAD)
            scores = lax.dot_general(qa[at, here], ka[:, here], (((1,), (1,)), ((), ())),
                                     preferred_element_type=F32)
            top = jnp.max(scores, axis=1, keepdims=True)
            expo = jnp.exp2((scores - top) * factor)
            total = jnp.sum(expo, axis=1, keepdims=True)
            out = jnp.dot(expo.astype(BF16), va[:, here], preferred_element_type=F32) / total
            oa[at, here] = out.astype(BF16)
        if i < pairs - 1:
            for part in range(2):
                back_copy(2 * j + part).start()
        else:
            back_copy(s + 1 - 2 * lax.rem(s, 2)).start()
    ar[:, span(s, width)] = oa[span(s, rows), :]

    arrived(4, 5)
    pass_on(13, place(xo, zh), whole, far, dev_z)
    pass_on(14, place(xo, zh), whole, every, dev_core)

    finish(hlocal)
    for offset in range(1, n_seq):
        back_copy(lax.rem(s + offset, n_seq)).wait()
    step = jnp.full((1, 1), steps[t], jnp.int32).astype(F32)
    level = 1.0 - step / SAMPLE_STEPS
    level = 5.0 * level / (1.0 + 4.0 * level)
    reward = jnp.zeros((1, 1), F32)
    for c in range(n_seq):
        here = slice(c * width, (c + 1) * width)
        value = (hidden[:, here].astype(F32) + ar[:, here].astype(F32)).astype(BF16)
        final[:, here] = value
        value = value.astype(F32)
        part = jnp.sum(value * head[:, here], axis=0, keepdims=True)
        reward = reward + jnp.sum(part, axis=1, keepdims=True)
        noised = ((1.0 - level) * value + level * noise[:, here].astype(F32)).astype(BF16)
        noisy[:, here] = noised
        nt[here, :] = noised.T
    mine[...] = jnp.broadcast_to(reward / math.sqrt(length), mine.shape)
    rcopies = share("seq", n_seq, mine, rslots, r1s, r1r)

    def slices(j, part, dst, peer):
        offset = lax.rem(peer - t + n_fsdp, n_fsdp)
        return remote(part.at[feat(peer), :], dst.at[:, span(t, rows)], send.at[j, offset],
                      recv.at[j, offset], "fsdp", peer)

    def spread(j, part, dst):
        copies = []
        for offset in range(1, n_fsdp):
            peer = lax.rem(t + offset, n_fsdp)
            copy = remote(part, dst, send.at[j, offset], recv.at[j, offset], "fsdp", peer)
            copy.start()
            copies.append(copy)
        return copies

    for offset in range(1, n_fsdp):
        slices(0, nt, na, lax.rem(t + offset, n_fsdp)).start()
    na[:, span(t, rows)] = nt[feat(t), :]

    tile = (features + RANK) // 5

    def multiply(a, b, start=False):
        here = span(a * 2 + b, 2 * nr)
        for c in range(5):
            cols = slice(c * tile, (c + 1) * tile)
            part = jnp.dot(noisy[:, here], wb[here, cols], preferred_element_type=F32)
            acc[:, cols] = part if start else acc[:, cols] + part

    arrived(3)
    multiply(x, zh, True)
    arrived(6, 7)
    pass_on(15, place(xm, zz), first, near, dev_xp)
    pass_on(16, place(xp, zz), second, near, dev_xm)
    pass_on(17, place(xm, zz), whole, near, dev_core)
    pass_on(18, place(xp, zz), whole, near, dev_core)
    finish(rcopies)
    total = rslots[0]
    for c in range(1, n_seq):
        total = total + rslots[c]
    mine[...] = total
    rcopies = share("fsdp", n_fsdp, mine, rewards, r2s, r2r)
    arrived(10)
    multiply(xm, zh)
    arrived(11)
    multiply(xp, zh)
    arrived(8, 9)
    pass_on(19, place(xm, zz), whole, far, dev_core)
    pass_on(20, place(xp, zz), whole, far, dev_core)
    arrived(12)
    multiply(x, zz)
    arrived(14)
    multiply(xo, zh)
    arrived(13, 15, 16)
    pass_on(21, place(xo, zz), whole, every, dev_core)
    arrived(17, 19)
    multiply(xm, zz)
    arrived(18, 20)
    multiply(xp, zz)
    finish(rcopies)
    lane = lax.broadcasted_iota(jnp.int32, (1, 128), 1)
    reward = jnp.zeros((1, 128), F32)
    for c in range(n_fsdp):
        reward = jnp.where(lane == c, rewards[c, 0:1, :], reward)
    advantage = advantage_row(counts, reward, lane)
    advantage = jnp.sum(jnp.where(lane == t, advantage, 0.0), axis=1, keepdims=True)
    arrived(21)
    multiply(xo, zz)

    lowrank = acc[:, features:].astype(BF16)
    lows[1] = lowrank.T
    low_copies = spread(2, lows.at[1], la.at[1, :, span(t, rows)])
    la[1, :, span(t, rows)] = lows[1]
    loss = jnp.zeros((rows, 1), F32)
    back = jnp.zeros((rows, RANK), F32)
    chips = n_fsdp // 2
    for i in range(chips):
        j = lax.rem(t // 2 + 1 + i, chips)
        here = span(j, 2 * nr)
        up_rows = wb[here, features + RANK:]
        target = noise[:, here].astype(F32) - final[:, here].astype(F32)
        error = acc[:, here] + adapter_scale * lax.dot_general(
            lowrank, up_rows, (((1,), (1,)), ((), ())), preferred_element_type=F32) - target
        loss = loss + jnp.sum(error * error, axis=1, keepdims=True)
        slope = (advantage * error / length).astype(BF16)
        st[here, :] = slope.T
        if i < chips - 1:
            for part in range(2):
                slices(1, st, sa, 2 * j + part).start()
        else:
            slices(1, st, sa, t + 1 - 2 * core).start()
        back = back + jnp.dot(slope, up_rows, preferred_element_type=F32)
    sa[:, span(t, rows)] = st[feat(t), :]
    lows[0] = (adapter_scale * back).astype(BF16).T
    low_copies += spread(3, lows.at[0], la.at[0, :, span(t, rows)])
    la[0, :, span(t, rows)] = lows[0]
    token_loss = jnp.broadcast_to(advantage * loss / (features * rows), (rows, 128)).T
    sub = lax.broadcasted_iota(jnp.int32, (8, rows), 0)
    meta[...] = jnp.where(sub == 0, owners[...], token_loss[0:8, :])
    low_copies += spread(4, meta, ma.at[:, span(t, rows)])
    ma[:, span(t, rows)] = meta[...]

    lanes = lax.broadcasted_iota(jnp.int32, (8, 128), 1)
    batch = 4
    norms = jnp.zeros((8, 128), F32)
    finish(low_copies)
    for offset in range(1, n_fsdp):
        slices(0, nt, na, lax.rem(t + offset, n_fsdp)).wait()
        slices(1, st, sa, lax.rem(t + offset, n_fsdp)).wait()
    owner = ma[0:1, :]
    loss_out[...] = jnp.broadcast_to(
        jnp.sum(jnp.where(owner == t.astype(F32), ma[1:2, :], 0.0), axis=1, keepdims=True),
        loss_out.shape)
    for j, other in ((1, sa), (0, na)):
        for g in range(n_fsdp // batch):
            for e in range(batch):
                hot = jnp.where(owner == float(g * batch + e), 1.0, 0.0)
                hot = jnp.broadcast_to(hot, (16, owner.shape[1])).astype(BF16)
                for r in range(RANK // 16):
                    left[j, e * RANK + r * 16:e * RANK + r * 16 + 16, :] = (
                        la[j, r * 16:r * 16 + 16, :] * hot)
            prod = lax.dot_general(left[j], other[...], (((1,), (1,)), ((), ())),
                                   preferred_element_type=F32)
            if j == 1:
                prod = adapter_scale * prod
            for e in range(batch):
                piece = prod[e * RANK:(e + 1) * RANK]
                d = g * batch + e
                sh[d, j * RANK:(j + 1) * RANK, :] = piece
                square = jnp.sum(jnp.sum(piece * piece, axis=0, keepdims=True), axis=1, keepdims=True)
                norms = jnp.where(lanes == d, norms + square, norms)

    mine[...] = norms
    finish(share("fsdp", n_fsdp, mine, slots1, s1, r1))
    norms = slots1[0]
    for c in range(1, n_fsdp):
        norms = norms + slots1[c]
    mine[...] = norms
    finish(share("seq", n_seq, mine, slots2, s2, r2))
    total = slots2[0]
    for c in range(1, n_seq):
        total = total + slots2[c]
    square_total = jnp.sum(total[0:1, :], axis=1, keepdims=True)
    limit = jnp.sqrt(square_total / (n_fsdp * n_seq) + norm_eps)
    clip = limit / jnp.maximum(jnp.sqrt(norms[0:1, :]), limit)
    factors = [jnp.sum(jnp.where(lane == d, clip, 0.0), axis=1, keepdims=True) for d in range(n_fsdp)]
    for j in range(2):
        here = slice(j * RANK, (j + 1) * RANK)
        total = factors[0] * sh[0, here, :]
        for d in range(1, n_fsdp):
            total = total + factors[d] * sh[d, here, :]
        gt[:, here] = total.T

    copies = []
    for offset in range(1, n_seq):
        peer = lax.rem(s + offset, n_seq)
        copy = remote(gt.at[pl.ds(pl.multiple_of(peer * own, 8), own), :], gslots.at[s],
                      s3.at[offset], r3.at[offset], "seq", peer)
        copy.start()
        copies.append(copy)
    gslots[s] = gt[pl.ds(pl.multiple_of(s * own, 8), own), :]
    finish(copies)
    total = gslots[0]
    for c in range(1, n_seq):
        total = total + gslots[c]
    down_out[...] = total[:, :RANK]
    up_out[...] = total[:, RANK:]
    for i in range(len(wcopies)):
        wcopies[i].wait_send()


def per_device(
    incoming_hidden_state, projected_queries, projected_keys, projected_values, training_noise,
    group_trajectory_counts, timestep, block_shard_owner, frozen_weight, adapter_down_weight,
    adapter_up_weight, linear_reward_head,
):
    rows, features = incoming_hidden_state.shape[1:]
    n_seq = lax.axis_size("seq")
    n_fsdp = lax.axis_size("fsdp")
    width = features // n_seq
    part = features // n_fsdp
    own = part // n_seq
    length = rows * n_seq
    every = rows * n_fsdp
    owners = jnp.repeat(block_shard_owner[0, :, 0], ROWS_PER_BLOCK).astype(F32)[None, :]
    vmem = pl.BlockSpec(memory_space=pltpu.VMEM)
    smem = pl.BlockSpec(memory_space=pltpu.SMEM)
    hbm = pl.BlockSpec(memory_space=pl.ANY)
    dma = pltpu.SemaphoreType.DMA
    final, grad_down, grad_up, loss = pl.pallas_call(
        functools.partial(step_kernel, n_seq, n_fsdp),
        out_shape=(
            jax.ShapeDtypeStruct((rows, features), BF16),
            jax.ShapeDtypeStruct((own, RANK), F32),
            jax.ShapeDtypeStruct((own, RANK), F32),
            jax.ShapeDtypeStruct((8, 128), F32),
        ),
        in_specs=[hbm, hbm, hbm, hbm, hbm, smem, smem, vmem, hbm, hbm, hbm, vmem],
        out_specs=(vmem,) * 4,
        scratch_shapes=[
            pltpu.VMEM((rows, features), BF16),
            pltpu.VMEM((rows, features), BF16),
            pltpu.VMEM((features, features + 2 * RANK), BF16),
            pltpu.VMEM((length, width), BF16),
            pltpu.VMEM((length, width), BF16),
            pltpu.VMEM((length, width), BF16),
            pltpu.VMEM((length, width), BF16),
            pltpu.VMEM((rows, features), BF16),
            pltpu.VMEM((rows, features), BF16),
            pltpu.VMEM((rows, features + RANK), F32),
            pltpu.VMEM((features, rows), BF16),
            pltpu.VMEM((features, rows), BF16),
            pltpu.VMEM((part, every), BF16),
            pltpu.VMEM((part, every), BF16),
            pltpu.VMEM((2, RANK, every), BF16),
            pltpu.VMEM((8, every), F32),
            pltpu.VMEM((2, 4 * RANK, every), BF16),
            pltpu.VMEM((n_fsdp, 2 * RANK, part), F32),
            pltpu.VMEM((8, 128), F32),
            pltpu.VMEM((8, rows), F32),
            pltpu.VMEM((2, RANK, rows), BF16),
            pltpu.VMEM((n_seq, 8, 128), F32),
            pltpu.VMEM((n_fsdp, 8, 128), F32),
            pltpu.VMEM((n_fsdp, 8, 128), F32),
            pltpu.VMEM((n_seq, 8, 128), F32),
            pltpu.VMEM((part, 2 * RANK), F32),
            pltpu.VMEM((n_seq, own, 2 * RANK), F32),
            dma((3, n_seq)), dma((3, n_seq)), dma((8,)),
            dma((22,)), dma((22,)),
            dma((n_seq,)), dma((n_seq,)),
            dma((n_seq,)), dma((n_seq,)),
            dma((n_fsdp,)), dma((n_fsdp,)),
            dma((5, n_fsdp)), dma((5, n_fsdp)),
            dma((n_fsdp,)), dma((n_fsdp,)),
            dma((n_seq,)), dma((n_seq,)),
            dma((n_seq,)), dma((n_seq,)),
        ],
        compiler_params=pltpu.CompilerParams(
            collective_id=0, has_side_effects=True, vmem_limit_bytes=58 * 2**20
        ),
        cost_estimate=pl.CostEstimate(
            flops=10**10, bytes_accessed=8 * 2**20, transcendentals=3 * 2**20
        ),
    )(
        incoming_hidden_state[0], projected_queries[0], projected_keys[0], projected_values[0],
        training_noise[0], group_trajectory_counts, timestep, owners, frozen_weight,
        adapter_down_weight, adapter_up_weight, linear_reward_head[None, :],
    )
    return final[None], grad_down, grad_up, loss[:1, :1]


def solution(mesh):
    return jax.shard_map(
        per_device,
        mesh=mesh,
        in_specs=(
            P("fsdp", "seq", None),
            P("fsdp", "seq", None),
            P("fsdp", "seq", None),
            P("fsdp", "seq", None),
            P("fsdp", "seq", None),
            P(),
            P(),
            P("fsdp", "seq", None),
            P("fsdp", None),
            P("fsdp", None),
            P("fsdp", None),
            P(),
        ),
        out_specs=(
            P("fsdp", "seq", None),
            P(("fsdp", "seq"), None),
            P(("fsdp", "seq"), None),
            P("fsdp", "seq"),
        ),
        check_vma=False,
    )
```

```python
import functools
import math

import jax
import jax.numpy as jnp
from jax import lax
from jax.experimental import pallas as pl
from jax.experimental.pallas import tpu as pltpu
from jax.sharding import PartitionSpec as P

MESH = pl.DeviceIdType.MESH
BF16 = jnp.bfloat16
F32 = jnp.float32

HEAD = 128
ROWS_PER_BLOCK = 8
SAMPLE_STEPS = 16
RANK = 128
QUARTER = 128
QUARTER_AT = 0
CHIPS = ((2, 0), (1, 0), (3, 0), (2, 1), (1, 1), (3, 1), (0, 1))
COLUMNS = ((1, 0), (3, 0), (2, 1), (0, 1), (1, 1), (3, 1), (2, 0))
SPLIT = 1536

adapter_scale = 2.0
adv_floor = 0.5
norm_eps = 1e-06


def remote(src, dst, send, recv, axis, peer):
    return pltpu.make_async_remote_copy(
        src_ref=src, dst_ref=dst, send_sem=send, recv_sem=recv,
        device_id={axis: peer}, device_id_type=MESH,
    )


def share(axis, count, src, slots, send, recv):
    me = lax.axis_index(axis)
    copies = []
    for offset in range(1, count):
        peer = lax.rem(me + offset, count)
        copy = remote(src, slots.at[me], send.at[offset], recv.at[offset], axis, peer)
        copy.start()
        copies.append(copy)
    slots[me] = src[...]
    return copies


def finish(copies):
    for copy in copies:
        copy.wait()


def advantage_row(counts, rewards, lane):
    result = jnp.zeros_like(rewards)
    low = jnp.int32(0)
    for g in range(counts.shape[0]):
        high = low + counts[g]
        inside = jnp.where((lane >= low) & (lane < high), 1.0, 0.0)
        number = jnp.sum(inside, axis=1, keepdims=True)
        mean = jnp.sum(inside * rewards, axis=1, keepdims=True) / number
        dev = inside * (rewards - mean)
        spread = jnp.sqrt(jnp.sum(dev * dev, axis=1, keepdims=True) / number)
        result = result + dev / jnp.maximum(spread, adv_floor)
        low = high
    return result


def step_kernel(
    n_seq, n_fsdp,
    hidden_in, q, k, v, noise_in, counts_in, steps_in, owners_in, frozen, down, up, head_in,
    final_out, down_out, up_out, loss_out,
    counts, steps, owners, head, final, hidden, noise, wb, qa, ka, va, oa, ar, noisy, acc, nt, st, na, sa, la, ma, left, sh,
    mine, meta, lows, rslots, rewards, slots1, slots2, gt, gslots,
    ksend, krecv, klocal, wsend, wrecv, bsend, brecv, r1s, r1r, r2s, r2r,
    send, recv, lsend, lrecv, s1, r1, s2, r2, s3, r3,
):
    t = lax.axis_index("fsdp")
    s = lax.axis_index("seq")
    rows, features = q.shape
    width = features // n_seq
    length = rows * n_seq
    heads = width // HEAD
    nr = frozen.shape[0]
    nc = wb.shape[3]
    base = 4 * QUARTER
    own = nr // n_seq
    x, zh, core = t // 4, lax.rem(t // 2, 2), lax.rem(t, 2)
    xp, xm, xo, zz = lax.rem(x + 1, 4), lax.rem(x + 3, 4), lax.rem(x + 2, 4), 1 - zh

    def place(a, b):
        return a * 4 + b * 2 + core

    dev_xp, dev_xm = (place(xp, zh), s), (place(xm, zh), s)
    dev_z = (place(x, zz), lax.rem(s + n_seq // 2, n_seq))
    dev_core = (x * 4 + zh * 2 + 1 - core, s)
    y, zl = lax.rem(s, 4), s // 4
    yp, ym, yo = lax.rem(y + 1, 4), lax.rem(y + 3, 4), lax.rem(y + 2, 4)
    dev_yp, dev_ym = (t, zl * 4 + yp), (t, zl * 4 + ym)

    barrier = pltpu.get_barrier_semaphore()
    for axis, count, me in (("seq", n_seq, s), ("fsdp", n_fsdp, t)):
        for offset in range(1, count):
            pl.semaphore_signal(barrier, inc=1, device_id={axis: lax.rem(me + offset, count)},
                                device_id_type=MESH)
    pl.semaphore_signal(barrier, inc=1, device_id=dev_z, device_id_type=MESH)

    def span(i, size):
        return pl.ds(pl.multiple_of(i * size, 128), size)

    def feat(i):
        return pl.ds(pl.multiple_of(i * nr, 16), nr)

    wlocal = []
    for j, (part, at, size) in enumerate(((frozen, 0, features), (down, features, RANK),
                                          (up, features + RANK, RANK))):
        wlocal.append(pltpu.make_async_copy(part, wb.at[t // 2, core, :, pl.ds(at, size)], klocal.at[j]))
    klocals = []
    for j, (part, dst) in enumerate(((k, ka), (q, qa), (v, va))):
        klocals.append(pltpu.make_async_copy(part.at[:, span(s, width)], dst.at[span(s, rows), :],
                                             klocal.at[3 + j]))
    hlocal = [pltpu.make_async_copy(hidden_in, hidden, klocal.at[6]),
              pltpu.make_async_copy(noise_in, noise, klocal.at[7]),
              pltpu.make_async_copy(head_in, head, klocal.at[8]),
              pltpu.make_async_copy(counts_in, counts, klocal.at[9]),
              pltpu.make_async_copy(steps_in, steps, klocal.at[10]),
              pltpu.make_async_copy(owners_in, owners, klocal.at[11])]
    for copy in wlocal + klocals + hlocal:
        copy.start()
    pl.semaphore_wait(barrier, n_seq + n_fsdp - 1)

    kcopies = []

    def scatter(j, part, dst):
        for dy, dz in COLUMNS:
            peer = lax.rem(zl + dz, 2) * 4 + lax.rem(y + dy, 4)
            offset = dz * 4 + dy
            copy = remote(part.at[:, span(peer, width)], dst.at[span(s, rows), :],
                          ksend.at[j, offset], krecv.at[j, offset], "seq", peer)
            copy.start()
            kcopies.append(copy)

    half = nr // 2
    whole, first, second = (0, nr), (0, half), (half, half)
    every, near, far = (base, nc - base), (base, SPLIT), (base + SPLIT, nc - base - SPLIT)
    mine_y = (pl.multiple_of(y * QUARTER, 128), QUARTER)
    wcopies = {}

    def start(i, ref, device):
        wcopies[i] = pltpu.make_async_remote_copy(
            src_ref=ref, dst_ref=ref, send_sem=wsend.at[i], recv_sem=wrecv.at[i],
            device_id=device, device_id_type=MESH)
        wcopies[i].start()

    def pass_on(i, block, part, columns, device):
        start(i, wb.at[block // 2, core, pl.ds(part[0], part[1]), pl.ds(columns[0], columns[1])],
              device)

    def quarter(i, j, device, chips=(0, 8)):
        start(i, wb.at[pl.ds(chips[0], chips[1]), core, :,
                       pl.ds(pl.multiple_of(j * QUARTER, 128), QUARTER)], device)

    def arrived(*which):
        for i in which:
            wcopies[i].wait_recv()

    scatter(0, k, ka)
    finish(wlocal)
    pass_on(22, t, whole, mine_y, dev_z)
    pass_on(23, t, whole, mine_y, dev_xp)
    pass_on(24, t, whole, mine_y, dev_xm)
    pass_on(0, t, first, every, dev_xp)
    pass_on(1, t, second, every, dev_xm)
    pass_on(2, t, whole, every, dev_z)
    pass_on(3, t, whole, every, dev_core)
    scatter(1, q, qa)
    scatter(2, v, va)

    arrived(22)
    pass_on(25, place(x, zz), whole, mine_y, dev_xp)
    pass_on(26, place(x, zz), whole, mine_y, dev_xm)
    arrived(23, 24)
    pass_on(27, place(xm, zh), first, mine_y, dev_xp)
    pass_on(28, place(xp, zh), second, mine_y, dev_xm)
    pass_on(39, t, second, every, dev_xp)
    pass_on(40, t, first, every, dev_xm)
    arrived(25, 26)
    pass_on(29, place(xm, zz), first, mine_y, dev_xp)
    pass_on(30, place(xp, zz), second, mine_y, dev_xm)
    arrived(0, 1)
    pass_on(4, place(xm, zh), first, every, dev_xp)
    pass_on(5, place(xp, zh), second, every, dev_xm)
    arrived(2)
    pass_on(6, place(x, zz), whole, near, dev_xp)
    pass_on(7, place(x, zz), whole, near, dev_xm)
    arrived(39, 40)
    pass_on(8, place(xm, zh), whole, far, dev_z)
    pass_on(9, place(xp, zh), whole, far, dev_z)
    pass_on(10, place(xm, zh), whole, every, dev_core)
    pass_on(11, place(xp, zh), whole, every, dev_core)
    pass_on(12, place(x, zz), whole, every, dev_core)

    finish(klocals + kcopies)
    factor = math.log2(math.e) / math.sqrt(HEAD)
    pairs = n_seq // 2

    def back_copy(peer):
        offset = lax.rem(peer - s + n_seq, n_seq)
        return remote(oa.at[span(peer, rows), :], ar.at[:, span(s, width)], bsend.at[offset],
                      brecv.at[offset], "seq", peer)

    for i in range(pairs):
        j = lax.rem(s // 2 + 1 + i, pairs)
        at = span(j, 2 * rows)
        for h in range(heads):
            here = slice(h * HEAD, (h + 1) * HEAD)
            scores = lax.dot_general(qa[at, here], ka[:, here], (((1,), (1,)), ((), ())),
                                     preferred_element_type=F32)
            top = jnp.max(scores, axis=1, keepdims=True)
            expo = jnp.exp2((scores - top) * factor)
            total = jnp.sum(expo, axis=1, keepdims=True)
            out = jnp.dot(expo.astype(BF16), va[:, here], preferred_element_type=F32) / total
            oa[at, here] = out.astype(BF16)
        if i < pairs - 1:
            for part in range(2):
                back_copy(2 * j + part).start()
        if i == QUARTER_AT:
            arrived(27, 28, 29, 30)
            quarter(31, y, dev_yp)
            quarter(32, y, dev_ym)
            quarter(33, y, dev_core)
        if i < pairs - 1:
            pass
        else:
            back_copy(s + 1 - 2 * lax.rem(s, 2)).start()
    ar[:, span(s, width)] = oa[span(s, rows), :]

    arrived(4, 5)
    pass_on(13, place(xo, zh), whole, far, dev_z)
    pass_on(14, place(xo, zh), whole, every, dev_core)

    finish(hlocal)
    for offset in range(1, n_seq):
        back_copy(lax.rem(s + offset, n_seq)).wait()
    step = jnp.full((1, 1), steps[t], jnp.int32).astype(F32)
    level = 1.0 - step / SAMPLE_STEPS
    level = 5.0 * level / (1.0 + 4.0 * level)
    reward = jnp.zeros((1, 1), F32)
    for c in range(n_seq):
        here = slice(c * width, (c + 1) * width)
        value = (hidden[:, here].astype(F32) + ar[:, here].astype(F32)).astype(BF16)
        final[:, here] = value
        value = value.astype(F32)
        part = jnp.sum(value * head[:, here], axis=0, keepdims=True)
        reward = reward + jnp.sum(part, axis=1, keepdims=True)
        noised = ((1.0 - level) * value + level * noise[:, here].astype(F32)).astype(BF16)
        noisy[:, here] = noised
        nt[here, :] = noised.T
    final_copy = pltpu.make_async_copy(final, final_out, klocal.at[12])
    final_copy.start()
    mine[...] = jnp.broadcast_to(reward / math.sqrt(length), mine.shape)
    rcopies = share("seq", n_seq, mine, rslots, r1s, r1r)

    chips = n_fsdp // 2
    seat = span(core * chips + t // 2, rows)

    def chip(dx, dz):
        return lax.rem(x + dx, 4) * 2 + lax.rem(zh + dz, 2)

    def slices(j, part, dst, dx, dz, dc):
        peer = chip(dx, dz) * 2 + lax.rem(core + dc, 2)
        offset = (dx * 2 + dz) * 2 + dc
        return remote(part.at[feat(peer), :], dst.at[:, seat], send.at[j, offset],
                      recv.at[j, offset], "fsdp", peer)

    others = [(dx, dz, dc) for dx, dz in CHIPS for dc in range(2)] + [(0, 0, 1)]

    def to_chips(j):
        copies = []
        for dx, dz in CHIPS:
            peer = chip(dx, dz) * 2 + core
            offset = dx * 2 + dz
            copy = remote(lows.at[j], la.at[j, core, :, span(t // 2, rows)], lsend.at[j, offset],
                          lrecv.at[j, offset], "fsdp", peer)
            copy.start()
            copies.append(copy)
        la[j, core, :, span(t // 2, rows)] = lows[j]
        return copies

    def to_core(j):
        copy = remote(la.at[j, core], la.at[j, core], lsend.at[j, 0], lrecv.at[j, 0], "fsdp",
                      t + 1 - 2 * core)
        copy.start()
        return [copy]

    def spread(j, part, dst):
        copies = []
        for offset in range(1, n_fsdp):
            peer = lax.rem(t + offset, n_fsdp)
            copy = remote(part, dst, send.at[j, offset], recv.at[j, offset], "fsdp", peer)
            copy.start()
            copies.append(copy)
        return copies


    tiles = [(c, min(512, features + RANK - c)) for c in range(base, features + RANK, 512)]

    def multiply(a, b, start=False):
        here = span(a * 2 + b, 2 * nr)
        for at, size in tiles:
            cols = slice(at, at + size)
            rhs = wb[a * 2 + b, :, :, cols].reshape(2 * nr, size)
            part = jnp.dot(noisy[:, here], rhs, preferred_element_type=F32)
            acc[:, cols] = part if start else acc[:, cols] + part

    def multiply_quarter(j):
        cols = pl.ds(pl.multiple_of(j * QUARTER, 128), QUARTER)
        rhs = wb[:, :, :, cols].reshape(features, QUARTER)
        acc[:, cols] = jnp.dot(noisy[...], rhs, preferred_element_type=F32)

    arrived(31, 32)
    quarter(34, ym, dev_yp, (0, 4))
    quarter(35, yp, dev_ym, (4, 4))
    quarter(36, ym, dev_core)
    quarter(37, yp, dev_core)
    arrived(3)
    multiply(x, zh, True)
    arrived(6, 7)
    pass_on(15, place(xm, zz), first, near, dev_xp)
    pass_on(16, place(xp, zz), second, near, dev_xm)
    pass_on(17, place(xm, zz), whole, near, dev_core)
    pass_on(18, place(xp, zz), whole, near, dev_core)
    for other in others:
        slices(0, nt, na, *other).start()
    na[:, seat] = nt[feat(t), :]
    finish(rcopies)
    total = rslots[0]
    for c in range(1, n_seq):
        total = total + rslots[c]
    mine[...] = total
    rcopies = share("fsdp", n_fsdp, mine, rewards, r2s, r2r)
    arrived(10)
    multiply(xm, zh)
    arrived(11)
    multiply(xp, zh)
    arrived(8, 9)
    pass_on(19, place(xm, zz), whole, far, dev_core)
    pass_on(20, place(xp, zz), whole, far, dev_core)
    arrived(12)
    multiply(x, zz)
    arrived(14)
    multiply(xo, zh)
    arrived(33)
    multiply_quarter(y)
    arrived(13, 15, 16)
    pass_on(21, place(xo, zz), whole, every, dev_core)
    arrived(36)
    multiply_quarter(ym)
    arrived(37)
    multiply_quarter(yp)
    arrived(34, 35)
    quarter(38, yo, dev_core)
    arrived(17, 19)
    multiply(xm, zz)
    arrived(18, 20)
    multiply(xp, zz)
    finish(rcopies)
    lane = lax.broadcasted_iota(jnp.int32, (1, 128), 1)
    reward = jnp.zeros((1, 128), F32)
    for c in range(n_fsdp):
        reward = jnp.where(lane == c, rewards[c, 0:1, :], reward)
    advantage = advantage_row(counts, reward, lane)
    advantage = jnp.sum(jnp.where(lane == t, advantage, 0.0), axis=1, keepdims=True)
    arrived(21)
    multiply(xo, zz)
    arrived(38)
    multiply_quarter(yo)

    lowrank = acc[:, features:].astype(BF16)
    lows[1] = lowrank.T
    low_copies = to_chips(1)
    loss = jnp.zeros((rows, 1), F32)
    back = jnp.zeros((rows, RANK), F32)
    for dx, dz in CHIPS + ((0, 0),):
        j = chip(dx, dz)
        here = span(j, 2 * nr)
        up_rows = wb[j, :, :, features + RANK:].reshape(2 * nr, RANK)
        target = noise[:, here].astype(F32) - final[:, here].astype(F32)
        error = acc[:, here] + adapter_scale * lax.dot_general(
            lowrank, up_rows, (((1,), (1,)), ((), ())), preferred_element_type=F32) - target
        loss = loss + jnp.sum(error * error, axis=1, keepdims=True)
        slope = (advantage * error / length).astype(BF16)
        st[here, :] = slope.T
        for dc in range(0 if dx or dz else 1, 2):
            slices(1, st, sa, dx, dz, dc).start()
        back = back + jnp.dot(slope, up_rows, preferred_element_type=F32)
    sa[:, seat] = st[feat(t), :]
    lows[0] = (adapter_scale * back).astype(BF16).T
    back_copies = to_chips(0)
    token_loss = jnp.broadcast_to(advantage * loss / (features * rows), (rows, 128)).T
    sub = lax.broadcasted_iota(jnp.int32, (8, rows), 0)
    of_token = lax.broadcasted_iota(jnp.int32, (8, rows), 1) // ROWS_PER_BLOCK
    named = jnp.zeros((8, rows), jnp.int32)
    for b in range(rows // ROWS_PER_BLOCK):
        named = jnp.where(of_token == b, owners[b], named)
    named = named.astype(F32)
    meta[...] = jnp.where(sub == 0, named, token_loss[0:8, :])
    meta_copies = spread(2, meta, ma.at[:, seat])
    ma[:, seat] = meta[...]

    lanes = lax.broadcasted_iota(jnp.int32, (8, 128), 1)
    batch = 4
    norms = jnp.zeros((8, 128), F32)
    finish(low_copies)
    low_copies = to_core(1)
    finish(meta_copies)
    owner = ma[0:1, :]
    loss_out[...] = jnp.broadcast_to(
        jnp.sum(jnp.where(owner == t.astype(F32), ma[1:2, :], 0.0), axis=1, keepdims=True),
        loss_out.shape)

    def shards(j, g, other, norms):
        for e in range(batch):
            hot = jnp.where(owner == float(g * batch + e), 1.0, 0.0)
            hot = jnp.broadcast_to(hot, (16, owner.shape[1])).astype(BF16)
            for c in range(2):
                cols = slice(c * chips * rows, (c + 1) * chips * rows)
                for r in range(RANK // 16):
                    left[j, e * RANK + r * 16:e * RANK + r * 16 + 16, cols] = (
                        la[j, c, r * 16:r * 16 + 16, :] * hot[:, cols])
        prod = lax.dot_general(left[j], other[...], (((1,), (1,)), ((), ())),
                               preferred_element_type=F32)
        if j == 1:
            prod = adapter_scale * prod
        for e in range(batch):
            piece = prod[e * RANK:(e + 1) * RANK]
            d = g * batch + e
            sh[d, j * RANK:(j + 1) * RANK, :] = piece
            square = jnp.sum(jnp.sum(piece * piece, axis=0, keepdims=True), axis=1, keepdims=True)
            norms = jnp.where(lanes == d, norms + square, norms)
        return norms

    for other in others:
        slices(1, st, sa, *other).wait()
    finish(back_copies)
    back_copies = to_core(0)
    finish(low_copies)
    for g in range(n_fsdp // batch):
        norms = shards(1, g, sa, norms)
    for other in others:
        slices(0, nt, na, *other).wait()
    finish(back_copies)
    for g in range(n_fsdp // batch):
        norms = shards(0, g, na, norms)

    mine[...] = norms
    finish(share("fsdp", n_fsdp, mine, slots1, s1, r1))
    norms = slots1[0]
    for c in range(1, n_fsdp):
        norms = norms + slots1[c]
    mine[...] = norms
    finish(share("seq", n_seq, mine, slots2, s2, r2))
    total = slots2[0]
    for c in range(1, n_seq):
        total = total + slots2[c]
    square_total = jnp.sum(total[0:1, :], axis=1, keepdims=True)
    limit = jnp.sqrt(square_total / (n_fsdp * n_seq) + norm_eps)
    clip = limit / jnp.maximum(jnp.sqrt(norms[0:1, :]), limit)
    factors = [jnp.sum(jnp.where(lane == d, clip, 0.0), axis=1, keepdims=True) for d in range(n_fsdp)]
    for j in range(2):
        here = slice(j * RANK, (j + 1) * RANK)
        total = factors[0] * sh[0, here, :]
        for d in range(1, n_fsdp):
            total = total + factors[d] * sh[d, here, :]
        gt[:, here] = total.T

    copies = []
    for offset in range(1, n_seq):
        peer = lax.rem(s + offset, n_seq)
        copy = remote(gt.at[pl.ds(pl.multiple_of(peer * own, 8), own), :], gslots.at[s],
                      s3.at[offset], r3.at[offset], "seq", peer)
        copy.start()
        copies.append(copy)
    gslots[s] = gt[pl.ds(pl.multiple_of(s * own, 8), own), :]
    finish(copies)
    total = gslots[0]
    for c in range(1, n_seq):
        total = total + gslots[c]
    down_out[...] = total[:, :RANK]
    up_out[...] = total[:, RANK:]
    for i in range(len(wcopies)):
        wcopies[i].wait_send()
    final_copy.wait()


def hand_over_kernel(final_in, down_in, up_in, loss_in, final, down_out, up_out, loss_out):
    final[...] = final_in[...]
    down_out[...] = down_in[...]
    up_out[...] = up_in[...]
    loss_out[...] = loss_in[0:1, 0:1]


def hand_over(final, grad_down, grad_up, loss):
    vmem = pl.BlockSpec(memory_space=pltpu.VMEM)
    return pl.pallas_call(
        hand_over_kernel,
        out_shape=(
            jax.ShapeDtypeStruct(final.shape, final.dtype),
            jax.ShapeDtypeStruct(grad_down.shape, F32),
            jax.ShapeDtypeStruct(grad_up.shape, F32),
            jax.ShapeDtypeStruct((1, 1), F32),
        ),
        in_specs=[vmem] * 4,
        out_specs=(vmem,) * 4,
    )(final, grad_down, grad_up, loss)


def per_device(
    incoming_hidden_state, projected_queries, projected_keys, projected_values, training_noise,
    group_trajectory_counts, timestep, block_shard_owner, frozen_weight, adapter_down_weight,
    adapter_up_weight, linear_reward_head,
):
    rows, features = incoming_hidden_state.shape[1:]
    n_seq = lax.axis_size("seq")
    n_fsdp = lax.axis_size("fsdp")
    width = features // n_seq
    part = features // n_fsdp
    own = part // n_seq
    length = rows * n_seq
    every = rows * n_fsdp
    vmem = pl.BlockSpec(memory_space=pltpu.VMEM)
    hbm = pl.BlockSpec(memory_space=pl.ANY)
    dma = pltpu.SemaphoreType.DMA
    final, grad_down, grad_up, loss = pl.pallas_call(
        functools.partial(step_kernel, n_seq, n_fsdp),
        out_shape=(
            jax.ShapeDtypeStruct((rows, features), BF16),
            jax.ShapeDtypeStruct((own, RANK), F32),
            jax.ShapeDtypeStruct((own, RANK), F32),
            jax.ShapeDtypeStruct((8, 128), F32),
        ),
        in_specs=[hbm] * 12,
        out_specs=(hbm, vmem, vmem, vmem),
        scratch_shapes=[
            pltpu.SMEM(group_trajectory_counts.shape, jnp.int32),
            pltpu.SMEM(timestep.shape, jnp.int32),
            pltpu.SMEM((rows // ROWS_PER_BLOCK,), jnp.int32),
            pltpu.VMEM((1, features), F32),
            pltpu.VMEM((rows, features), BF16),
            pltpu.VMEM((rows, features), BF16),
            pltpu.VMEM((rows, features), BF16),
            pltpu.VMEM((n_fsdp // 2, 2, part, features + 2 * RANK), BF16),
            pltpu.VMEM((length, width), BF16),
            pltpu.VMEM((length, width), BF16),
            pltpu.VMEM((length, width), BF16),
            pltpu.VMEM((length, width), BF16),
            pltpu.VMEM((rows, features), BF16),
            pltpu.VMEM((rows, features), BF16),
            pltpu.VMEM((rows, features + RANK), F32),
            pltpu.VMEM((features, rows), BF16),
            pltpu.VMEM((features, rows), BF16),
            pltpu.VMEM((part, every), BF16),
            pltpu.VMEM((part, every), BF16),
            pltpu.VMEM((2, 2, RANK, every // 2), BF16),
            pltpu.VMEM((8, every), F32),
            pltpu.VMEM((2, 4 * RANK, every), BF16),
            pltpu.VMEM((n_fsdp, 2 * RANK, part), F32),
            pltpu.VMEM((8, 128), F32),
            pltpu.VMEM((8, rows), F32),
            pltpu.VMEM((2, RANK, rows), BF16),
            pltpu.VMEM((n_seq, 8, 128), F32),
            pltpu.VMEM((n_fsdp, 8, 128), F32),
            pltpu.VMEM((n_fsdp, 8, 128), F32),
            pltpu.VMEM((n_seq, 8, 128), F32),
            pltpu.VMEM((part, 2 * RANK), F32),
            pltpu.VMEM((n_seq, own, 2 * RANK), F32),
            dma((3, n_seq)), dma((3, n_seq)), dma((13,)),
            dma((41,)), dma((41,)),
            dma((n_seq,)), dma((n_seq,)),
            dma((n_seq,)), dma((n_seq,)),
            dma((n_fsdp,)), dma((n_fsdp,)),
            dma((3, n_fsdp)), dma((3, n_fsdp)),
            dma((2, n_fsdp // 2)), dma((2, n_fsdp // 2)),
            dma((n_fsdp,)), dma((n_fsdp,)),
            dma((n_seq,)), dma((n_seq,)),
            dma((n_seq,)), dma((n_seq,)),
        ],
        compiler_params=pltpu.CompilerParams(
            collective_id=0, has_side_effects=True, vmem_limit_bytes=58 * 2**20
        ),
        cost_estimate=pl.CostEstimate(
            flops=10**10, bytes_accessed=8 * 2**20, transcendentals=3 * 2**20
        ),
    )(
        incoming_hidden_state[0], projected_queries[0], projected_keys[0], projected_values[0],
        training_noise[0], group_trajectory_counts, timestep, block_shard_owner[0, :, 0], frozen_weight,
        adapter_down_weight, adapter_up_weight, linear_reward_head[None, :],
    )
    final, grad_down, grad_up, loss = hand_over(final, grad_down, grad_up, loss)
    return final[None], grad_down, grad_up, loss


def solution(mesh):
    return jax.shard_map(
        per_device,
        mesh=mesh,
        in_specs=(
            P("fsdp", "seq", None),
            P("fsdp", "seq", None),
            P("fsdp", "seq", None),
            P("fsdp", "seq", None),
            P("fsdp", "seq", None),
            P(),
            P(),
            P("fsdp", "seq", None),
            P("fsdp", None),
            P("fsdp", None),
            P("fsdp", None),
            P(),
        ),
        out_specs=(
            P("fsdp", "seq", None),
            P(("fsdp", "seq"), None),
            P(("fsdp", "seq"), None),
            P("fsdp", "seq"),
        ),
        check_vma=False,
    )
```

```python
import functools
import math

import jax
import jax.numpy as jnp
from jax import lax
from jax.experimental import pallas as pl
from jax.experimental.pallas import tpu as pltpu
from jax.sharding import PartitionSpec as P

MESH = pl.DeviceIdType.MESH
BF16 = jnp.bfloat16
F32 = jnp.float32

HEAD = 128
ROWS_PER_BLOCK = 8
SAMPLE_STEPS = 16
RANK = 128
QUARTER = 128
QUARTER_AT = 0
CHIPS = ((2, 0), (1, 0), (3, 0), (2, 1), (1, 1), (3, 1), (0, 1))
COLUMNS = ((1, 0), (3, 0), (2, 1), (0, 1), (1, 1), (3, 1), (2, 0))
SPLIT = 1536

adapter_scale = 2.0
adv_floor = 0.5
norm_eps = 1e-06


def remote(src, dst, send, recv, axis, peer):
    return pltpu.make_async_remote_copy(
        src_ref=src, dst_ref=dst, send_sem=send, recv_sem=recv,
        device_id={axis: peer}, device_id_type=MESH,
    )


def share(axis, count, src, slots, send, recv):
    me = lax.axis_index(axis)
    copies = []
    for offset in range(1, count):
        peer = lax.rem(me + offset, count)
        copy = remote(src, slots.at[me], send.at[offset], recv.at[offset], axis, peer)
        copy.start()
        copies.append(copy)
    slots[me] = src[...]
    return copies


def finish(copies):
    for copy in copies:
        copy.wait()


def advantage_row(counts, rewards, lane):
    result = jnp.zeros_like(rewards)
    low = jnp.int32(0)
    for g in range(counts.shape[0]):
        high = low + counts[g]
        inside = jnp.where((lane >= low) & (lane < high), 1.0, 0.0)
        number = jnp.sum(inside, axis=1, keepdims=True)
        mean = jnp.sum(inside * rewards, axis=1, keepdims=True) / number
        dev = inside * (rewards - mean)
        spread = jnp.sqrt(jnp.sum(dev * dev, axis=1, keepdims=True) / number)
        result = result + dev / jnp.maximum(spread, adv_floor)
        low = high
    return result


def step_kernel(
    n_seq, n_fsdp,
    hidden_in, q, k, v, noise_in, counts_in, steps_in, owners_in, frozen, down, up, head_in,
    final_out, down_out, up_out, loss_out,
    counts, steps, owners, head, final, hidden, noise, wb, qa, ka, va, oa, ar, noisy, acc, nt, st, na, sa, la, ma, left, sh,
    mine, meta, lows, rslots, rewards, slots1, slots2, gt, gslots,
    ksend, krecv, klocal, wsend, wrecv, bsend, brecv, r1s, r1r, r2s, r2r,
    send, recv, lsend, lrecv, s1, r1, s2, r2, s3, r3,
):
    t = lax.axis_index("fsdp")
    s = lax.axis_index("seq")
    rows, features = q.shape
    width = features // n_seq
    length = rows * n_seq
    heads = width // HEAD
    nr = frozen.shape[0]
    nc = wb.shape[3]
    base = 4 * QUARTER
    own = nr // n_seq
    x, zh, core = t // 4, lax.rem(t // 2, 2), lax.rem(t, 2)
    xp, xm, xo, zz = lax.rem(x + 1, 4), lax.rem(x + 3, 4), lax.rem(x + 2, 4), 1 - zh

    def place(a, b):
        return a * 4 + b * 2 + core

    dev_xp, dev_xm = (place(xp, zh), s), (place(xm, zh), s)
    dev_z = (place(x, zz), lax.rem(s + n_seq // 2, n_seq))
    dev_core = (x * 4 + zh * 2 + 1 - core, s)
    y, zl = lax.rem(s, 4), s // 4
    yp, ym, yo = lax.rem(y + 1, 4), lax.rem(y + 3, 4), lax.rem(y + 2, 4)
    dev_yp, dev_ym = (t, zl * 4 + yp), (t, zl * 4 + ym)

    barrier = pltpu.get_barrier_semaphore()
    for axis, count, me in (("seq", n_seq, s), ("fsdp", n_fsdp, t)):
        for offset in range(1, count):
            pl.semaphore_signal(barrier, inc=1, device_id={axis: lax.rem(me + offset, count)},
                                device_id_type=MESH)
    pl.semaphore_signal(barrier, inc=1, device_id=dev_z, device_id_type=MESH)

    def span(i, size):
        return pl.ds(pl.multiple_of(i * size, 128), size)

    def feat(i):
        return pl.ds(pl.multiple_of(i * nr, 16), nr)

    wlocal = []
    for j, (part, at, size) in enumerate(((frozen, 0, features), (down, features, RANK),
                                          (up, features + RANK, RANK))):
        wlocal.append(pltpu.make_async_copy(part, wb.at[t // 2, core, :, pl.ds(at, size)], klocal.at[j]))
    klocals = []
    for j, (part, dst) in enumerate(((k, ka), (q, qa), (v, va))):
        klocals.append(pltpu.make_async_copy(part.at[:, span(s, width)], dst.at[span(s, rows), :],
                                             klocal.at[3 + j]))
    hlocal = [pltpu.make_async_copy(hidden_in, hidden, klocal.at[6]),
              pltpu.make_async_copy(noise_in, noise, klocal.at[7]),
              pltpu.make_async_copy(head_in, head, klocal.at[8]),
              pltpu.make_async_copy(counts_in, counts, klocal.at[9]),
              pltpu.make_async_copy(steps_in, steps, klocal.at[10]),
              pltpu.make_async_copy(owners_in, owners, klocal.at[11])]
    for copy in wlocal + klocals + hlocal:
        copy.start()
    pl.semaphore_wait(barrier, n_seq + n_fsdp - 1)

    kcopies = []

    def scatter(j, part, dst):
        for dy, dz in COLUMNS:
            peer = lax.rem(zl + dz, 2) * 4 + lax.rem(y + dy, 4)
            offset = dz * 4 + dy
            copy = remote(part.at[:, span(peer, width)], dst.at[span(s, rows), :],
                          ksend.at[j, offset], krecv.at[j, offset], "seq", peer)
            copy.start()
            kcopies.append(copy)

    half = nr // 2
    whole, first, second = (0, nr), (0, half), (half, half)
    every, near, far = (base, nc - base), (base, SPLIT), (base + SPLIT, nc - base - SPLIT)
    mine_y = (pl.multiple_of(y * QUARTER, 128), QUARTER)
    wcopies = {}

    def start(i, ref, device):
        wcopies[i] = pltpu.make_async_remote_copy(
            src_ref=ref, dst_ref=ref, send_sem=wsend.at[i], recv_sem=wrecv.at[i],
            device_id=device, device_id_type=MESH)
        wcopies[i].start()

    def pass_on(i, block, part, columns, device):
        start(i, wb.at[block // 2, core, pl.ds(part[0], part[1]), pl.ds(columns[0], columns[1])],
              device)

    def quarter(i, j, device, chips=(0, 8)):
        start(i, wb.at[pl.ds(chips[0], chips[1]), core, :,
                       pl.ds(pl.multiple_of(j * QUARTER, 128), QUARTER)], device)

    def arrived(*which):
        for i in which:
            wcopies[i].wait_recv()

    scatter(0, k, ka)
    finish(wlocal)
    pass_on(22, t, whole, mine_y, dev_z)
    pass_on(23, t, whole, mine_y, dev_xp)
    pass_on(24, t, whole, mine_y, dev_xm)
    pass_on(0, t, first, every, dev_xp)
    pass_on(1, t, second, every, dev_xm)
    pass_on(2, t, whole, every, dev_z)
    pass_on(3, t, whole, every, dev_core)
    scatter(1, q, qa)
    scatter(2, v, va)

    arrived(22)
    pass_on(25, place(x, zz), whole, mine_y, dev_xp)
    pass_on(26, place(x, zz), whole, mine_y, dev_xm)
    arrived(23, 24)
    pass_on(27, place(xm, zh), first, mine_y, dev_xp)
    pass_on(28, place(xp, zh), second, mine_y, dev_xm)
    pass_on(39, t, second, every, dev_xp)
    pass_on(40, t, first, every, dev_xm)
    arrived(25, 26)
    pass_on(29, place(xm, zz), first, mine_y, dev_xp)
    pass_on(30, place(xp, zz), second, mine_y, dev_xm)
    arrived(0, 1)
    pass_on(4, place(xm, zh), first, every, dev_xp)
    pass_on(5, place(xp, zh), second, every, dev_xm)
    arrived(2)
    pass_on(6, place(x, zz), whole, near, dev_xp)
    pass_on(7, place(x, zz), whole, near, dev_xm)
    arrived(39, 40)
    pass_on(8, place(xm, zh), whole, far, dev_z)
    pass_on(9, place(xp, zh), whole, far, dev_z)
    pass_on(10, place(xm, zh), whole, every, dev_core)
    pass_on(11, place(xp, zh), whole, every, dev_core)
    pass_on(12, place(x, zz), whole, every, dev_core)

    finish(klocals + kcopies)
    factor = math.log2(math.e) / math.sqrt(HEAD)
    pairs = n_seq // 2

    def back_copy(peer):
        offset = lax.rem(peer - s + n_seq, n_seq)
        return remote(oa.at[span(peer, rows), :], ar.at[:, span(s, width)], bsend.at[offset],
                      brecv.at[offset], "seq", peer)

    for i in range(pairs):
        j = lax.rem(s // 2 + 1 + i, pairs)
        at = span(j, 2 * rows)
        for h in range(heads):
            here = slice(h * HEAD, (h + 1) * HEAD)
            scores = lax.dot_general(qa[at, here], ka[:, here], (((1,), (1,)), ((), ())),
                                     preferred_element_type=F32)
            top = jnp.max(scores, axis=1, keepdims=True)
            expo = jnp.exp2((scores - top) * factor)
            total = jnp.sum(expo, axis=1, keepdims=True)
            out = jnp.dot(expo.astype(BF16), va[:, here], preferred_element_type=F32) / total
            oa[at, here] = out.astype(BF16)
        if i < pairs - 1:
            for part in range(2):
                back_copy(2 * j + part).start()
        if i == QUARTER_AT:
            arrived(27, 28, 29, 30)
            quarter(31, y, dev_yp)
            quarter(32, y, dev_ym)
            quarter(33, y, dev_core)
        if i < pairs - 1:
            pass
        else:
            back_copy(s + 1 - 2 * lax.rem(s, 2)).start()
    ar[:, span(s, width)] = oa[span(s, rows), :]

    arrived(4, 5)
    pass_on(13, place(xo, zh), whole, far, dev_z)
    pass_on(14, place(xo, zh), whole, every, dev_core)

    finish(hlocal)
    for offset in range(1, n_seq):
        back_copy(lax.rem(s + offset, n_seq)).wait()
    step = jnp.full((1, 1), steps[t], jnp.int32).astype(F32)
    level = 1.0 - step / SAMPLE_STEPS
    level = 5.0 * level / (1.0 + 4.0 * level)
    reward = jnp.zeros((1, 1), F32)
    for c in range(n_seq):
        here = slice(c * width, (c + 1) * width)
        value = (hidden[:, here].astype(F32) + ar[:, here].astype(F32)).astype(BF16)
        final[:, here] = value
        value = value.astype(F32)
        part = jnp.sum(value * head[:, here], axis=0, keepdims=True)
        reward = reward + jnp.sum(part, axis=1, keepdims=True)
        noised = ((1.0 - level) * value + level * noise[:, here].astype(F32)).astype(BF16)
        noisy[:, here] = noised
        nt[here, :] = noised.T
    final_copy = pltpu.make_async_copy(final, final_out, klocal.at[12])
    final_copy.start()
    mine[...] = jnp.broadcast_to(reward / math.sqrt(length), mine.shape)
    rcopies = share("seq", n_seq, mine, rslots, r1s, r1r)

    chips = n_fsdp // 2
    seat = span(core * chips + t // 2, rows)

    def chip(dx, dz):
        return lax.rem(x + dx, 4) * 2 + lax.rem(zh + dz, 2)

    def slices(j, part, dst, dx, dz, dc):
        peer = chip(dx, dz) * 2 + lax.rem(core + dc, 2)
        offset = (dx * 2 + dz) * 2 + dc
        return remote(part.at[feat(peer), :], dst.at[:, seat], send.at[j, offset],
                      recv.at[j, offset], "fsdp", peer)

    others = [(dx, dz, dc) for dx, dz in CHIPS for dc in range(2)] + [(0, 0, 1)]

    def to_chips(j):
        copies = []
        for dx, dz in CHIPS:
            peer = chip(dx, dz) * 2 + core
            offset = dx * 2 + dz
            copy = remote(lows.at[j], la.at[j, core, :, span(t // 2, rows)], lsend.at[j, offset],
                          lrecv.at[j, offset], "fsdp", peer)
            copy.start()
            copies.append(copy)
        la[j, core, :, span(t // 2, rows)] = lows[j]
        return copies

    def to_core(j):
        copy = remote(la.at[j, core], la.at[j, core], lsend.at[j, 0], lrecv.at[j, 0], "fsdp",
                      t + 1 - 2 * core)
        copy.start()
        return [copy]

    def spread(j, part, dst):
        copies = []
        for offset in range(1, n_fsdp):
            peer = lax.rem(t + offset, n_fsdp)
            copy = remote(part, dst, send.at[j, offset], recv.at[j, offset], "fsdp", peer)
            copy.start()
            copies.append(copy)
        return copies


    tiles = [(c, min(512, features + RANK - c)) for c in range(base, features + RANK, 512)]

    def multiply(a, b, start=False):
        here = span(a * 2 + b, 2 * nr)
        for at, size in tiles:
            cols = slice(at, at + size)
            rhs = wb[a * 2 + b, :, :, cols].reshape(2 * nr, size)
            part = jnp.dot(noisy[:, here], rhs, preferred_element_type=F32)
            acc[:, cols] = part if start else acc[:, cols] + part

    def multiply_quarter(j):
        cols = pl.ds(pl.multiple_of(j * QUARTER, 128), QUARTER)
        rhs = wb[:, :, :, cols].reshape(features, QUARTER)
        acc[:, cols] = jnp.dot(noisy[...], rhs, preferred_element_type=F32)

    arrived(31, 32)
    quarter(34, ym, dev_yp, (0, 4))
    quarter(35, yp, dev_ym, (4, 4))
    quarter(36, ym, dev_core)
    quarter(37, yp, dev_core)
    arrived(3)
    multiply(x, zh, True)
    arrived(6, 7)
    pass_on(15, place(xm, zz), first, near, dev_xp)
    pass_on(16, place(xp, zz), second, near, dev_xm)
    pass_on(17, place(xm, zz), whole, near, dev_core)
    pass_on(18, place(xp, zz), whole, near, dev_core)
    for other in others:
        slices(0, nt, na, *other).start()
    na[:, seat] = nt[feat(t), :]
    finish(rcopies)
    total = rslots[0]
    for c in range(1, n_seq):
        total = total + rslots[c]
    mine[...] = total
    rcopies = share("fsdp", n_fsdp, mine, rewards, r2s, r2r)
    arrived(10)
    multiply(xm, zh)
    arrived(11)
    multiply(xp, zh)
    arrived(8, 9)
    pass_on(19, place(xm, zz), whole, far, dev_core)
    pass_on(20, place(xp, zz), whole, far, dev_core)
    arrived(12)
    multiply(x, zz)
    arrived(14)
    multiply(xo, zh)
    arrived(33)
    multiply_quarter(y)
    arrived(13)
    pass_on(41, place(xo, zz), whole, far, dev_core)
    arrived(15, 16)
    pass_on(21, place(xo, zz), whole, near, dev_core)
    arrived(36)
    multiply_quarter(ym)
    arrived(37)
    multiply_quarter(yp)
    arrived(34, 35)
    quarter(38, yo, dev_core)
    arrived(17, 19)
    multiply(xm, zz)
    arrived(18, 20)
    multiply(xp, zz)
    finish(rcopies)
    lane = lax.broadcasted_iota(jnp.int32, (1, 128), 1)
    reward = jnp.zeros((1, 128), F32)
    for c in range(n_fsdp):
        reward = jnp.where(lane == c, rewards[c, 0:1, :], reward)
    advantage = advantage_row(counts, reward, lane)
    advantage = jnp.sum(jnp.where(lane == t, advantage, 0.0), axis=1, keepdims=True)
    arrived(21, 41)
    multiply(xo, zz)
    arrived(38)
    multiply_quarter(yo)

    lowrank = acc[:, features:].astype(BF16)
    lows[1] = lowrank.T
    low_copies = to_chips(1)
    loss = jnp.zeros((rows, 1), F32)
    back = jnp.zeros((rows, RANK), F32)
    for dx, dz in CHIPS + ((0, 0),):
        j = chip(dx, dz)
        here = span(j, 2 * nr)
        up_rows = wb[j, :, :, features + RANK:].reshape(2 * nr, RANK)
        target = noise[:, here].astype(F32) - final[:, here].astype(F32)
        error = acc[:, here] + adapter_scale * lax.dot_general(
            lowrank, up_rows, (((1,), (1,)), ((), ())), preferred_element_type=F32) - target
        loss = loss + jnp.sum(error * error, axis=1, keepdims=True)
        slope = (advantage * error / length).astype(BF16)
        st[here, :] = slope.T
        for dc in range(0 if dx or dz else 1, 2):
            slices(1, st, sa, dx, dz, dc).start()
        back = back + jnp.dot(slope, up_rows, preferred_element_type=F32)
    sa[:, seat] = st[feat(t), :]
    lows[0] = (adapter_scale * back).astype(BF16).T
    back_copies = to_chips(0)
    token_loss = jnp.broadcast_to(advantage * loss / (features * rows), (rows, 128)).T
    sub = lax.broadcasted_iota(jnp.int32, (8, rows), 0)
    of_token = lax.broadcasted_iota(jnp.int32, (8, rows), 1) // ROWS_PER_BLOCK
    named = jnp.zeros((8, rows), jnp.int32)
    for b in range(rows // ROWS_PER_BLOCK):
        named = jnp.where(of_token == b, owners[b], named)
    named = named.astype(F32)
    meta[...] = jnp.where(sub == 0, named, token_loss[0:8, :])
    meta_copies = spread(2, meta, ma.at[:, seat])
    ma[:, seat] = meta[...]

    lanes = lax.broadcasted_iota(jnp.int32, (8, 128), 1)
    batch = 4
    norms = jnp.zeros((8, 128), F32)
    finish(low_copies)
    low_copies = to_core(1)
    finish(meta_copies)
    owner = ma[0:1, :]
    loss_out[...] = jnp.broadcast_to(
        jnp.sum(jnp.where(owner == t.astype(F32), ma[1:2, :], 0.0), axis=1, keepdims=True),
        loss_out.shape)

    def shards(j, g, other, norms):
        for e in range(batch):
            hot = jnp.where(owner == float(g * batch + e), 1.0, 0.0)
            hot = jnp.broadcast_to(hot, (16, owner.shape[1])).astype(BF16)
            for c in range(2):
                cols = slice(c * chips * rows, (c + 1) * chips * rows)
                for r in range(RANK // 16):
                    left[j, e * RANK + r * 16:e * RANK + r * 16 + 16, cols] = (
                        la[j, c, r * 16:r * 16 + 16, :] * hot[:, cols])
        prod = lax.dot_general(left[j], other[...], (((1,), (1,)), ((), ())),
                               preferred_element_type=F32)
        if j == 1:
            prod = adapter_scale * prod
        for e in range(batch):
            piece = prod[e * RANK:(e + 1) * RANK]
            d = g * batch + e
            sh[d, j * RANK:(j + 1) * RANK, :] = piece
            square = jnp.sum(jnp.sum(piece * piece, axis=0, keepdims=True), axis=1, keepdims=True)
            norms = jnp.where(lanes == d, norms + square, norms)
        return norms

    for other in others:
        slices(1, st, sa, *other).wait()
    finish(back_copies)
    back_copies = to_core(0)
    finish(low_copies)
    for g in range(n_fsdp // batch):
        norms = shards(1, g, sa, norms)
    for other in others:
        slices(0, nt, na, *other).wait()
    finish(back_copies)
    for g in range(n_fsdp // batch):
        norms = shards(0, g, na, norms)

    mine[...] = norms
    finish(share("fsdp", n_fsdp, mine, slots1, s1, r1))
    norms = slots1[0]
    for c in range(1, n_fsdp):
        norms = norms + slots1[c]
    mine[...] = norms
    finish(share("seq", n_seq, mine, slots2, s2, r2))
    total = slots2[0]
    for c in range(1, n_seq):
        total = total + slots2[c]
    square_total = jnp.sum(total[0:1, :], axis=1, keepdims=True)
    limit = jnp.sqrt(square_total / (n_fsdp * n_seq) + norm_eps)
    clip = limit / jnp.maximum(jnp.sqrt(norms[0:1, :]), limit)
    factors = [jnp.sum(jnp.where(lane == d, clip, 0.0), axis=1, keepdims=True) for d in range(n_fsdp)]
    for j in range(2):
        here = slice(j * RANK, (j + 1) * RANK)
        total = factors[0] * sh[0, here, :]
        for d in range(1, n_fsdp):
            total = total + factors[d] * sh[d, here, :]
        gt[:, here] = total.T

    copies = []
    for offset in range(1, n_seq):
        peer = lax.rem(s + offset, n_seq)
        copy = remote(gt.at[pl.ds(pl.multiple_of(peer * own, 8), own), :], gslots.at[s],
                      s3.at[offset], r3.at[offset], "seq", peer)
        copy.start()
        copies.append(copy)
    gslots[s] = gt[pl.ds(pl.multiple_of(s * own, 8), own), :]
    finish(copies)
    total = gslots[0]
    for c in range(1, n_seq):
        total = total + gslots[c]
    down_out[...] = total[:, :RANK]
    up_out[...] = total[:, RANK:]
    for i in range(len(wcopies)):
        wcopies[i].wait_send()
    final_copy.wait()


def hand_over_kernel(final_in, down_in, up_in, loss_in, final, down_out, up_out, loss_out):
    final[...] = final_in[...]
    down_out[...] = down_in[...]
    up_out[...] = up_in[...]
    loss_out[...] = loss_in[0:1, 0:1]


def hand_over(final, grad_down, grad_up, loss):
    rows, features = final.shape
    part = pl.BlockSpec((rows // 4, features), lambda i: (i, 0))

    def whole(shape):
        return pl.BlockSpec(shape, lambda i: (0, 0))

    shape = grad_down.shape
    return pl.pallas_call(
        hand_over_kernel,
        out_shape=(
            jax.ShapeDtypeStruct(final.shape, final.dtype),
            jax.ShapeDtypeStruct(grad_down.shape, F32),
            jax.ShapeDtypeStruct(grad_up.shape, F32),
            jax.ShapeDtypeStruct((1, 1), F32),
        ),
        grid=(4,),
        in_specs=[part, whole(shape), whole(shape), whole(loss.shape)],
        out_specs=(part, whole(shape), whole(shape), whole((1, 1))),
    )(final, grad_down, grad_up, loss)


def per_device(
    incoming_hidden_state, projected_queries, projected_keys, projected_values, training_noise,
    group_trajectory_counts, timestep, block_shard_owner, frozen_weight, adapter_down_weight,
    adapter_up_weight, linear_reward_head,
):
    rows, features = incoming_hidden_state.shape[1:]
    n_seq = lax.axis_size("seq")
    n_fsdp = lax.axis_size("fsdp")
    width = features // n_seq
    part = features // n_fsdp
    own = part // n_seq
    length = rows * n_seq
    every = rows * n_fsdp
    vmem = pl.BlockSpec(memory_space=pltpu.VMEM)
    hbm = pl.BlockSpec(memory_space=pl.ANY)
    dma = pltpu.SemaphoreType.DMA
    final, grad_down, grad_up, loss = pl.pallas_call(
        functools.partial(step_kernel, n_seq, n_fsdp),
        out_shape=(
            jax.ShapeDtypeStruct((rows, features), BF16),
            jax.ShapeDtypeStruct((own, RANK), F32),
            jax.ShapeDtypeStruct((own, RANK), F32),
            jax.ShapeDtypeStruct((8, 128), F32),
        ),
        in_specs=[hbm] * 12,
        out_specs=(hbm, vmem, vmem, vmem),
        scratch_shapes=[
            pltpu.SMEM(group_trajectory_counts.shape, jnp.int32),
            pltpu.SMEM(timestep.shape, jnp.int32),
            pltpu.SMEM((rows // ROWS_PER_BLOCK,), jnp.int32),
            pltpu.VMEM((1, features), F32),
            pltpu.VMEM((rows, features), BF16),
            pltpu.VMEM((rows, features), BF16),
            pltpu.VMEM((rows, features), BF16),
            pltpu.VMEM((n_fsdp // 2, 2, part, features + 2 * RANK), BF16),
            pltpu.VMEM((length, width), BF16),
            pltpu.VMEM((length, width), BF16),
            pltpu.VMEM((length, width), BF16),
            pltpu.VMEM((length, width), BF16),
            pltpu.VMEM((rows, features), BF16),
            pltpu.VMEM((rows, features), BF16),
            pltpu.VMEM((rows, features + RANK), F32),
            pltpu.VMEM((features, rows), BF16),
            pltpu.VMEM((features, rows), BF16),
            pltpu.VMEM((part, every), BF16),
            pltpu.VMEM((part, every), BF16),
            pltpu.VMEM((2, 2, RANK, every // 2), BF16),
            pltpu.VMEM((8, every), F32),
            pltpu.VMEM((2, 4 * RANK, every), BF16),
            pltpu.VMEM((n_fsdp, 2 * RANK, part), F32),
            pltpu.VMEM((8, 128), F32),
            pltpu.VMEM((8, rows), F32),
            pltpu.VMEM((2, RANK, rows), BF16),
            pltpu.VMEM((n_seq, 8, 128), F32),
            pltpu.VMEM((n_fsdp, 8, 128), F32),
            pltpu.VMEM((n_fsdp, 8, 128), F32),
            pltpu.VMEM((n_seq, 8, 128), F32),
            pltpu.VMEM((part, 2 * RANK), F32),
            pltpu.VMEM((n_seq, own, 2 * RANK), F32),
            dma((3, n_seq)), dma((3, n_seq)), dma((13,)),
            dma((42,)), dma((42,)),
            dma((n_seq,)), dma((n_seq,)),
            dma((n_seq,)), dma((n_seq,)),
            dma((n_fsdp,)), dma((n_fsdp,)),
            dma((3, n_fsdp)), dma((3, n_fsdp)),
            dma((2, n_fsdp // 2)), dma((2, n_fsdp // 2)),
            dma((n_fsdp,)), dma((n_fsdp,)),
            dma((n_seq,)), dma((n_seq,)),
            dma((n_seq,)), dma((n_seq,)),
        ],
        compiler_params=pltpu.CompilerParams(
            collective_id=0, has_side_effects=True, vmem_limit_bytes=58 * 2**20
        ),
        cost_estimate=pl.CostEstimate(
            flops=10**10, bytes_accessed=8 * 2**20, transcendentals=3 * 2**20
        ),
    )(
        incoming_hidden_state[0], projected_queries[0], projected_keys[0], projected_values[0],
        training_noise[0], group_trajectory_counts, timestep, block_shard_owner[0, :, 0], frozen_weight,
        adapter_down_weight, adapter_up_weight, linear_reward_head[None, :],
    )
    final, grad_down, grad_up, loss = hand_over(final, grad_down, grad_up, loss)
    return final[None], grad_down, grad_up, loss


def solution(mesh):
    return jax.shard_map(
        per_device,
        mesh=mesh,
        in_specs=(
            P("fsdp", "seq", None),
            P("fsdp", "seq", None),
            P("fsdp", "seq", None),
            P("fsdp", "seq", None),
            P("fsdp", "seq", None),
            P(),
            P(),
            P("fsdp", "seq", None),
            P("fsdp", None),
            P("fsdp", None),
            P("fsdp", None),
            P(),
        ),
        out_specs=(
            P("fsdp", "seq", None),
            P(("fsdp", "seq"), None),
            P(("fsdp", "seq"), None),
            P("fsdp", "seq"),
        ),
        check_vma=False,
    )
```
